32 devices in a mesh: leaf: 8 (over z, y), grid: 4 (over x, core).
Axes of the slice: x: 2, y: 2, z: 4, core: 2. Of those that a mesh axis runs over, the one named last changes fastest.
Arguments:
- rhs: bfloat16 [5, 16, 256, 256], P(None, 'leaf', 'grid'), may hold values from -6 to 6
- fwd_inv: bfloat16 [5, 16, 256, 256], P(None, 'leaf', 'grid')
- bwd_inv: bfloat16 [5, 16, 256, 256], P(None, 'leaf', 'grid')
- upd_t: bfloat16 [4, 16, 256, 512], P(None, 'leaf', 'grid'), may hold values from -0.25 to 0.25
- bwd_t: bfloat16 [4, 16, 512, 256], P(None, 'leaf', 'grid'), may hold values from -0.1875 to 0.1875
- dest_owner: int32 [4, 8, 4, 256, 1], P(None, 'leaf', 'grid'), may hold values from 0 to 7; in each aligned block of 256 rows (0 to 255, 256 to 511, ..., all dimensions but the last counted through in order) at most 85 rows name the same one
- dest_row: int32 [4, 8, 4, 256], P(None, 'leaf', 'grid'), may hold values from 128 to 639, as said below
Outputs:
- solution: bfloat16 [5, 16, 256, 256], P(None, 'leaf', 'grid')
The draws below stay inside these ranges and needn't reach their ends.
Inputs may be any that keep to these rules, and one draw needn't show every extreme that they name: `dest_owner`: in the rows of one device at one level (one aligned block of 256), no owner is named more than 85 times, a bound that some block reaches. `dest_row`: an entry of level l reaches a row of a later level: it lies from (l + 1) * 2 * 64 to 639.
All inputs are finite; a program needn't handle non-finite values.
Results may differ from the reference program's by a relative error of at most 0.025.
Values may be sent and summed in bfloat16 or wider, within the bound.
No kernel may reach another device: no remote copies, remote signals or barrier semaphores. Data moves between devices by JAX's collectives and lax.ppermute only.
A program may use at most 64 MiB of HBM per device.

```python
import math
import jax
import jax.numpy as jnp
import numpy as np
from jax import lax

W = 256
NRHS = 256
R = 512
LEV = 5
K = 2
LEAVES = 8
GROUPS = 4
SUPER = 16
LEVM1 = 4
WG = 64
RG = 128
CAP = 85


def unit_blocks(key, salt):
    base_key = jax.random.fold_in(key, salt)
    identity_mat = (lax.broadcasted_iota(jnp.int32, (W, W), 0) == lax.broadcasted_iota(jnp.int32, (W, W), 1)).astype(jnp.float32)
    noise_part = jax.random.normal(base_key, (LEV, SUPER, W, W), jnp.float32) * (0.5 / math.sqrt(W))
    return (identity_mat + noise_part).astype(jnp.bfloat16)


def draw_fwd_inv(key, part):
    return unit_blocks(key, 11)


def draw_bwd_inv(key, part):
    return unit_blocks(key, 23)


def draw_dest_row(key, part):
    base_key = jax.random.fold_in(key, 37)
    lowest = ((jnp.arange(LEVM1, dtype=jnp.int32) + 1) * (K * WG)).reshape(LEVM1, 1, 1, 1)
    return jax.random.randint(base_key, (LEVM1, LEAVES, GROUPS, RG * K), lowest, LEV * K * WG, dtype=jnp.int32)


def levels(own_key, shape, shards, least, largest):
    def one(axis_at, blocks):
        steps = jax.random.uniform(jax.random.fold_in(jax.random.fold_in(own_key, 6), axis_at), (blocks,), jnp.float32, least / len(shards), largest / len(shards))
        return jnp.repeat(jnp.exp(steps), shape[axis_at] // blocks).reshape((-1,) + (1,) * (len(shape) - axis_at - 1))

    gain = one(*shards[0])
    for cut in shards[1:]:
        gain = gain * one(*cut)
    return gain


def shared_out(stream_key, own, number, rows, number_of, top, reach, lean):
    ranking = jax.random.permutation(stream_key, number_of)
    crowded, common = shares(number_of, rows * top, reach, lean, True), shares(number_of, rows * top, reach, lean, False)
    places = jnp.arange(number_of)

    def named(lengths, rotation):
        used = int((lengths > 0).sum())
        fixed = max(1, used // 4)
        passed = fixed + (places - fixed + rotation * (used - fixed)) % max(1, number_of - fixed)
        return jnp.zeros((number_of,), jnp.int32).at[ranking[jnp.where(places < fixed, places, passed)]].set(jnp.asarray(lengths, jnp.int32))

    lengths = jnp.where(number % 4 == 0, named(crowded, number // 4), named(common, number - number // 4 - 1))
    mixed = jax.random.permutation(jax.random.fold_in(own, 3), number_of)
    source_of, taker = mixed[0:number_of // 2 * 2:2], mixed[1:number_of // 2 * 2:2]
    margin = jnp.minimum(lengths[source_of] - 1, reach - lengths[taker]) // 2
    margin = jnp.where((source_of == ranking[0]) | (taker == ranking[0]) | (lengths[taker] == 0), 0, jnp.maximum(margin, 0))
    passed = jax.random.randint(jax.random.fold_in(own, 4), (number_of // 2,), 0, 1 << 20) % (margin + 1)
    lengths = lengths.at[source_of].add(-passed).at[taker].add(passed)
    items = jnp.searchsorted(jnp.cumsum(lengths), jnp.arange(rows * top), side="right").astype(jnp.int32)
    table = items.reshape(top, rows).T
    table = table[jax.random.permutation(jax.random.fold_in(own, 1), rows)]
    rotation = jax.random.randint(jax.random.fold_in(own, 2), (rows, 1), 0, top)
    return jnp.take_along_axis(table, (jnp.arange(top)[None, :] + rotation) % top, axis=1)


def shares(count, total, limit, slope, full):
    weights = [(1 << 20) // math.isqrt(grade ** slope) + 1 for grade in range(1, count + 1)]
    largest = limit if full else min(limit, max(-(-total // count), total * weights[0] // sum(weights)))
    least = 1 if total - largest >= count - 1 else 0
    given, rest = [largest] + [least] * (count - 1), total - largest - least * (count - 1)
    while rest > 0:
        candidates = [i for i in range(1, count) if given[i] < largest] or [i for i in range(1, count) if given[i] < limit]
        whole, budget = sum([weights[i] for i in candidates]), rest
        for i in candidates:
            more = min(limit - given[i], max(1, budget * weights[i] // whole), rest)
            given[i] = given[i] + more
            rest = rest - more
    return np.array(given)


def normal_values(key, dims, spread, reach, pieces=(), kind=jnp.bfloat16):
    array = jax.random.normal(key, dims, jnp.float32) * spread
    if len(pieces) > 0:
        array = levels(key, dims, pieces, -0.22, 0.18) * array
    return jnp.clip(array, min=-reach, max=reach).astype(kind)


def setup_inputs(seed: int = 0) -> dict:
    arg_keys = jax.random.split(jax.random.key(seed), 8)
    rhs = normal_values(arg_keys[0], (LEV, SUPER, W, NRHS), 1.0, 6.0, ((1, 8), (2, 4)))
    fwd_inv = draw_fwd_inv(jax.random.fold_in(arg_keys[7], 71), 0)
    bwd_inv = draw_bwd_inv(jax.random.fold_in(arg_keys[7], 71), 0)
    upd_t = normal_values(arg_keys[3], (LEVM1, SUPER, W, R), (2 * W) ** -0.5, 0.25, ((1, 8), (2, 4)))
    bwd_t = normal_values(arg_keys[4], (LEVM1, SUPER, R, W), (2 * R) ** -0.5, 0.1875, ((1, 8), (2, 4)))
    dest_owner_keys = jax.random.split(jax.random.fold_in(arg_keys[5], 1), LEVM1 * LEAVES * GROUPS * (RG * K) // (RG * K))
    dest_owner_turns = jax.random.permutation(jax.random.fold_in(arg_keys[5], 3), LEVM1 * LEAVES * GROUPS * (RG * K) // (RG * K))
    dest_owner = jax.vmap(lambda own, number: shared_out(jax.random.fold_in(arg_keys[5], 2), own, number, RG * K, LEAVES, 1, CAP, 2))(dest_owner_keys, dest_owner_turns).reshape((LEVM1, LEAVES, GROUPS, RG * K, 1))
    dest_row = draw_dest_row(jax.random.fold_in(arg_keys[7], 71), 0)
    return dict(rhs=rhs, fwd_inv=fwd_inv, bwd_inv=bwd_inv, upd_t=upd_t, bwd_t=bwd_t, dest_owner=dest_owner, dest_row=dest_row)


def widen(values):
    return lax.optimization_barrier(values).astype(jnp.float32)


def flat_targets(dest_owner, dest_row, level):
    owner_ids = dest_owner[level][..., 0]
    offsets = dest_row[level]
    group_ids = jnp.arange(GROUPS, dtype=jnp.int32)[None, :, None]
    level_to = offsets // (K * WG)
    super_to = owner_ids * K + (offsets // WG) % K
    row_to = group_ids * WG + offsets % WG
    return ((level_to * SUPER + super_to) * W + row_to).reshape(-1).astype(jnp.int32)


def to_routed(values):
    shaped = values.reshape(LEAVES, K, GROUPS, RG, NRHS)
    return jnp.transpose(shaped, (0, 2, 3, 1, 4)).reshape(-1, NRHS)


def from_routed(values):
    shaped = values.reshape(LEAVES, GROUPS, RG, K, NRHS)
    return jnp.transpose(shaped, (0, 3, 1, 2, 4)).reshape(SUPER, R, NRHS)


def reference(rhs, fwd_inv, bwd_inv, upd_t, bwd_t, dest_owner, dest_row):
    level_rows = SUPER * W
    accum = rhs.astype(jnp.float32).reshape(LEV * level_rows, NRHS)
    forward_out = []
    for level in range(LEV):
        block = accum[level * level_rows:(level + 1) * level_rows].reshape(SUPER, W, NRHS).astype(jnp.bfloat16)
        solved = jnp.einsum('swv,svn->swn', widen(fwd_inv[level]), widen(block))
        forward_out.append(solved)
        if level < LEV - 1:
            lowered = solved.astype(jnp.bfloat16)
            summed = jnp.zeros((SUPER, R, NRHS), jnp.float32)
            for group in range(GROUPS):
                lower_part = widen(upd_t[level][:, group * WG:(group + 1) * WG, :])
                term = jnp.einsum('swr,swn->srn', lower_part, widen(lowered[:, group * WG:(group + 1) * WG, :]))
                summed = summed + widen(term.astype(jnp.bfloat16))
            accum = accum.at[flat_targets(dest_owner, dest_row, level)].add(-to_routed(summed))
    solution = jnp.zeros((LEV * level_rows, NRHS), jnp.bfloat16)
    for level in reversed(range(LEV)):
        reduced = forward_out[level]
        if level < LEV - 1:
            pulled = from_routed(solution[flat_targets(dest_owner, dest_row, level)])
            for group in range(GROUPS):
                upper_rows = widen(bwd_t[level][:, group * RG:(group + 1) * RG, :])
                term = jnp.einsum('sjw,sjn->swn', upper_rows, widen(pulled[:, group * RG:(group + 1) * RG, :]))
                reduced = reduced - widen(term.astype(jnp.bfloat16))
        result = jnp.einsum('swv,svn->swn', widen(bwd_inv[level]), widen(reduced.astype(jnp.bfloat16)))
        solution = solution.at[level * level_rows:(level + 1) * level_rows].set(result.astype(jnp.bfloat16).reshape(level_rows, NRHS))
    return solution.reshape(LEV, SUPER, W, NRHS)
```

```python
import functools

import jax
import jax.numpy as jnp
from jax import lax
from jax.experimental import pallas as pl
from jax.experimental.pallas import tpu as pltpu
from jax.sharding import PartitionSpec as P

BF = jnp.bfloat16
F32 = jnp.float32
LANES = 128
ROWS_AT_ONCE = 256
VMEM_BYTES = 48 * 1024 * 1024


def nn(a, b):
    return lax.dot_general(a, b, (((1,), (0,)), ((), ())), preferred_element_type=F32)


def nt(a, b):
    return lax.dot_general(a, b, (((1,), (1,)), ((), ())), preferred_element_type=F32)


class Plan:
    def __init__(self, mesh, rhs, upd_t, bwd_t):
        self.levels, self.kept, self.rows, self.columns = rhs.shape
        self.leaves, self.groups = mesh.shape["leaf"], mesh.shape["grid"]
        self.parts = 2 if self.leaves % 2 == 0 else 1
        self.owners = self.leaves // self.parts
        self.supers = self.parts * self.kept
        self.chunk = self.columns // (self.groups * self.parts)
        self.width = self.rows * self.groups
        self.update_rows = upd_t.shape[3]
        self.group_rows = bwd_t.shape[2]
        self.slab = (self.supers * self.chunk, self.width)
        self.targets = self.supers * self.owners * self.rows
        self.sources = self.supers * self.group_rows
        self.blocks = [(dp, dg) for dp in range(self.parts) for dg in range(self.groups)]

    def place(self):
        leaf, grid = lax.axis_index("leaf"), lax.axis_index("grid")
        return leaf // self.parts, leaf % self.parts, grid


def fetch(plan, blocks, pieces, sems):
    _, part, grid = plan.place()
    copies = []
    for slab, make in pieces:
        group = []
        for ref, (dp, dg) in zip(blocks, plan.blocks):
            copy = pltpu.make_async_copy(
                ref.at[slab],
                make(part ^ dp, grid ^ dg),
                sems.at[len(copies) * len(plan.blocks) + len(group)],
            )
            copy.start()
            group.append(copy)
        copies.append(group)
    return copies


def wait(group):
    for copy in group:
        copy.wait()


def matrix(plan, ref, s):
    whole = ref[s // plan.kept, s % plan.kept]
    return whole.reshape(-1, whole.shape[-1])


def pick_columns(plan, ref):
    _, part, grid = plan.place()
    first = (part * plan.groups + grid) * plan.chunk
    shape = (plan.chunk, plan.columns)
    pick = lax.broadcasted_iota(jnp.int32, shape, 1) == first + lax.broadcasted_iota(jnp.int32, shape, 0)
    pick = jnp.where(pick, 1.0, 0.0).astype(BF)
    return jnp.concatenate([nt(pick, matrix(plan, ref, s)) for s in range(plan.supers)], axis=0)


def onehot(keys, first, rows):
    iota = lax.broadcasted_iota(jnp.int32, (rows, keys.shape[1]), 0)
    return jnp.where(iota == keys - first, 1.0, 0.0).astype(BF)


def cross(even, odd):
    half = even.shape[1] // 2
    low = lax.broadcasted_iota(jnp.int32, even.shape, 1) < half
    return (
        jnp.where(low, even, pltpu.roll(odd, half, 1)),
        jnp.where(low, pltpu.roll(even, half, 1), odd),
    )


def scatter(plan, sent, key_ref, level_to, emit):
    c, per = plan.chunk, max(1, ROWS_AT_ONCE // plan.rows)
    per = min(per, plan.owners)
    for pair in range(plan.groups // 2):
        given = []
        for g in (2 * pair, 2 * pair + 1):
            lanes = slice(g * plan.group_rows, (g + 1) * plan.group_rows)
            given.append(
                jnp.concatenate([sent[s * c : (s + 1) * c, lanes] for s in range(plan.supers)], axis=1)
            )
        for s in range(plan.supers):
            for first in range(0, plan.owners, per):
                row = level_to * plan.targets + (s * plan.owners + first) * plan.rows
                even, odd = [
                    nt(given[i], onehot(key_ref[2 * pair + i : 2 * pair + i + 1, :], row, per * plan.rows))
                    for i in range(2)
                ]
                for j in range(0, per, 2):
                    at = slice(j * plan.rows, (j + 2) * plan.rows)
                    one, two = cross(even[:, at], odd[:, at])
                    emit(first + j, s, pair, one)
                    emit(first + j + 1, s, pair, two)


def gather(plan, slabs, key_ref, level_from, g):
    c, pair = plan.chunk, g // 2
    lanes = slice(pair * LANES, (pair + 1) * LANES)
    total = None
    per = min(plan.owners, max(2, 4 * ROWS_AT_ONCE // plan.rows))
    for s in range(plan.supers):
        for first in range(0, plan.owners, per):
            given = []
            for d in range(first, first + per, 2):
                even, odd = [slabs[d + i][s * c : (s + 1) * c, lanes].astype(F32) for i in range(2)]
                given.append(cross(even, odd)[g % 2])
            row = level_from * plan.targets + (s * plan.owners + first) * plan.rows
            term = nn(
                jnp.concatenate(given, axis=1).astype(BF),
                onehot(key_ref[g : g + 1, :], row, per * plan.rows),
            )
            total = term if total is None else total + term
    return total


def forward_kernel(plan, level, part_of, fresh, added, *refs):
    refs = list(refs)
    key_ref = None if level == plan.levels - 1 else refs.pop(0)
    start_ref = None if fresh else refs.pop(0)
    arrived = [] if fresh else [refs.pop(0) for _ in range(plan.owners)]
    more_ref = refs.pop(0) if added else None
    blocks = [refs.pop(0) for _ in plan.blocks]
    out_ref = refs.pop(0)
    last = level == plan.levels - 1
    if last:
        solved_ref = refs.pop(0)
    else:
        sent_ref = refs.pop(0)
        slab_refs = [refs.pop(0) for _ in range(plan.owners)]
    if fresh:
        rhs_ref = refs.pop(0)
    inv_ref = refs.pop(0)
    if last:
        back_ref = refs.pop(0)
    else:
        upd_ref = refs.pop(0)
    sems = refs.pop(0)
    c = plan.chunk

    pieces = []
    if fresh:
        pieces.append((part_of["rhs"], lambda p, g: rhs_ref.at[p, :, g]))
    pieces.append((part_of["fwd"], lambda p, g: inv_ref.at[p, :, g]))
    if last:
        pieces.append((part_of["inv"], lambda p, g: back_ref.at[p, :, g]))
    else:
        for half in range(plan.update_rows // plan.width):
            pieces.append((part_of["upd"] + half, lambda p, g, half=half: upd_ref.at[half, p, :, g]))
    copies = fetch(plan, blocks, pieces, sems)

    if fresh:
        wait(copies.pop(0))
        block = pick_columns(plan, rhs_ref)
    else:
        block = start_ref[...] - arrived[0][...]
        for ref in arrived[1:]:
            block = block - ref[...].astype(F32)
    block = block.astype(BF)
    wait(copies.pop(0))
    solved = jnp.concatenate(
        [nt(block[s * c : (s + 1) * c], matrix(plan, inv_ref, s)) for s in range(plan.supers)], axis=0
    )
    out_ref[...] = solved
    lowered = solved.astype(BF)
    for group in copies:
        wait(group)
    if last:
        for s in range(plan.supers):
            at = slice(s * c, (s + 1) * c)
            solved_ref[at, :] = nt(lowered[at], matrix(plan, back_ref, s)).astype(BF)
        return
    for s in range(plan.supers):
        at = slice(s * c, (s + 1) * c)
        for half in range(plan.update_rows // plan.width):
            sent_ref[at, half * plan.width : (half + 1) * plan.width] = nn(
                lowered[at], matrix(plan, upd_ref.at[half], s)
            ).astype(BF)

    def emit(distance, s, pair, value):
        at, lanes = slice(s * c, (s + 1) * c), slice(pair * LANES, (pair + 1) * LANES)
        if more_ref is not None:
            value = value + more_ref[distance, at, lanes]
        slab_refs[distance][at, lanes] = value.astype(slab_refs[distance].dtype)

    scatter(plan, sent_ref[...], key_ref, level + 1, emit)


def ahead_kernel(plan, level, part_of, *refs):
    refs = list(refs)
    far = level < plan.levels - 1
    sent = [refs.pop(0) for _ in range(level)] if far else []
    key_refs = [refs.pop(0) for _ in sent]
    blocks = [refs.pop(0) for _ in plan.blocks]
    start_ref = refs.pop(0)
    more_ref = refs.pop(0) if far else None
    rhs_ref, sems = refs
    copies = fetch(plan, blocks, [(part_of["rhs"], lambda p, g: rhs_ref.at[p, :, g])], sems)
    c = plan.chunk
    for i, (ref, key_ref) in enumerate(zip(sent, key_refs)):

        def emit(distance, s, pair, value, first=i == 0):
            at, lanes = slice(s * c, (s + 1) * c), slice(pair * LANES, (pair + 1) * LANES)
            if not first:
                value = value + more_ref[distance, at, lanes]
            more_ref[distance, at, lanes] = value

        scatter(plan, ref[...], key_ref, level + 1, emit)
    wait(copies[0])
    start_ref[...] = pick_columns(plan, rhs_ref)


def known_kernel(plan, froms, *refs):
    key_ref, out_ref = refs[0], refs[-1]
    slabs = [refs[1 + i * plan.owners : 1 + (i + 1) * plan.owners] for i in range(len(froms))]
    for g in range(plan.groups):
        total = None
        for level_from, own in zip(froms, slabs):
            term = gather(plan, own, key_ref, level_from, g)
            total = term if total is None else total + term
        out_ref[g] = total.astype(BF)


def backward_kernel(plan, level, part_of, known, *refs):
    refs = list(refs)
    key_ref = refs.pop(0)
    slabs = [refs.pop(0) for _ in range(plan.owners)]
    known_ref = refs.pop(0) if known else None
    forward_ref = refs.pop(0)
    blocks = [refs.pop(0) for _ in plan.blocks]
    solved_ref, upper_ref, inv_ref, sems = refs
    c, half_rows = plan.chunk, plan.rows
    pieces = [
        (
            part_of["upper"] + h,
            lambda p, g, h=h: upper_ref.at[p, :, g, pl.ds(h * half_rows, half_rows)],
        )
        for h in range(plan.group_rows // half_rows)
    ]
    pieces.append((part_of["inv"], lambda p, g: inv_ref.at[p, :, g]))
    copies = fetch(plan, blocks, pieces, sems)
    pulled = []
    for g in range(plan.groups):
        found = gather(plan, slabs, key_ref, level + 1, g)
        if known:
            found = found + known_ref[g].astype(F32)
        pulled.append(found.astype(BF))
    for group in copies:
        wait(group)
    for s in range(plan.supers):
        at = slice(s * c, (s + 1) * c)
        lanes = slice(s * plan.group_rows, (s + 1) * plan.group_rows)
        upper = nn(jnp.concatenate([p[:, lanes] for p in pulled], axis=1), matrix(plan, upper_ref, s))
        reduced = (forward_ref[at, :] - upper).astype(BF)
        solved_ref[at, :] = nt(reduced, matrix(plan, inv_ref, s)).astype(BF)


def pieces_kernel(plan, *refs):
    _, part, grid = plan.place()
    slabs, outs = refs[: plan.levels], refs[plan.levels :]
    rows = plan.kept * plan.chunk
    for out, (dp, dg) in zip(outs, plan.blocks):
        first = pl.multiple_of((part ^ dp) * rows, rows)
        lane = pl.multiple_of((grid ^ dg) * plan.rows // LANES * LANES, LANES)
        for level, slab in enumerate(slabs):
            out[level] = slab[pl.ds(first, rows), pl.ds(lane, LANES)]


def result_kernel(plan, *refs):
    _, part, grid = plan.place()
    refs = list(refs)
    scratch, out = refs.pop(), refs.pop()
    c = plan.chunk
    shape = (plan.rows, LANES)
    lane = lax.broadcasted_iota(jnp.int32, shape, 1) - grid * plan.rows % LANES
    pick = jnp.where(lane == lax.broadcasted_iota(jnp.int32, shape, 0), 1.0, 0.0).astype(BF)
    for level in range(plan.levels):
        for k in range(plan.kept):
            for ref, (dp, dg) in zip(refs, plan.blocks):
                at = ((part ^ dp) * plan.groups + (grid ^ dg)) * c
                scratch[level, k, pl.ds(pl.multiple_of(at, c), c), :] = ref[level, k * c : (k + 1) * c, :]
    for level in range(plan.levels):
        for k in range(plan.kept):
            out[level, k] = nt(pick, scratch[level, k]).astype(BF)


VM = pl.BlockSpec(memory_space=pltpu.VMEM)
ANY = pl.BlockSpec(memory_space=pl.ANY)


def call(body, args, specs, outs, scratch, flops, moved):
    return pl.pallas_call(
        body,
        in_specs=specs,
        out_specs=[VM] * len(outs),
        out_shape=[jax.ShapeDtypeStruct(shape, dtype) for shape, dtype in outs],
        scratch_shapes=scratch,
        compiler_params=pltpu.CompilerParams(vmem_limit_bytes=VMEM_BYTES),
        cost_estimate=pl.CostEstimate(flops=flops, bytes_accessed=moved, transcendentals=0),
    )(*args)


def solve(plan, rhs, fwd_inv, bwd_inv, upd_t, bwd_t, dest_owner, dest_row):
    levels, owners = plan.levels, plan.owners
    owner_at, part, grid = plan.place()

    def over_leaf(x, step):
        return lax.ppermute(x, "leaf", [(i, i ^ step) for i in range(plan.leaves)])

    def over_grid(x, step):
        return lax.ppermute(x, "grid", [(i, i ^ step) for i in range(plan.groups)])

    per_owner = levels * plan.kept * plan.rows
    code = dest_owner.reshape(levels - 1, -1) * per_owner + dest_row.reshape(levels - 1, -1)
    pairs = [[i * plan.parts + j for j in range(plan.parts)] for i in range(owners)]
    code = lax.all_gather(code, "leaf", axis=0, axis_index_groups=pairs)
    code = lax.all_gather(code, "grid", axis=0)
    code = code.reshape(plan.groups, plan.parts, levels - 1, plan.group_rows, plan.kept)
    code = jnp.transpose(code, (2, 0, 1, 4, 3)).reshape(levels - 1, plan.groups, plan.sources)
    leaf_to, row_to = code // per_owner, code % per_owner
    super_to = leaf_to % plan.parts * plan.kept + row_to // plan.rows % plan.kept
    distance = (leaf_to // plan.parts) ^ owner_at
    keys = row_to // (plan.kept * plan.rows) * plan.targets
    keys = keys + (super_to * owners + distance) * plan.rows + row_to % plan.rows

    def cut(x):
        k, r, w = x.shape
        x = x.reshape(k, r // plan.rows, plan.rows, w // plan.width, plan.width)
        return jnp.transpose(x, (1, 3, 0, 2, 4)).reshape(-1, k, plan.rows, plan.width)

    where = {}

    def chunk(number, names):
        slabs, at = [], 0
        for name, level in names:
            array = dict(rhs=rhs, fwd=fwd_inv, inv=bwd_inv, upd=upd_t, upper=bwd_t)[name][level]
            slabs.append(cut(array))
            where[name, level] = (number, at)
            at += slabs[-1].shape[0]
        return jnp.concatenate(slabs, axis=0)

    def spread(own, by_leaf_last):
        got = {(0, 0): own}
        high = [1 << b for b in reversed(range(1, (plan.groups - 1).bit_length()))]
        if plan.parts > 1:
            got[1, 0] = over_leaf(own, 1)
        for step in high:
            for dg in [dg for dp, dg in got if dp == 0]:
                got[0, dg ^ step] = over_grid(got[0, dg], step)
                if plan.parts > 1:
                    if by_leaf_last:
                        got[1, dg ^ step] = over_leaf(got[0, dg ^ step], 1)
                    else:
                        got[1, dg ^ step] = over_grid(got[1, dg], step)
        if plan.groups > 1:
            for dp, dg in list(got):
                got[dp, dg ^ 1] = over_grid(got[dp, dg], 1)
        return [got[block] for block in plan.blocks]

    top = levels - 1
    names = [[("rhs", 0), ("fwd", 0), ("upd", 0)]]
    for level in range(1, top):
        names.append([("rhs", level), ("fwd", level), ("upd", level)])
    names[-1] += [("rhs", top), ("fwd", top), ("inv", top)]
    back = [[("upper", level), ("inv", level)] for level in reversed(range(top))]
    half = len(back) // 2
    names.append(sum(back[:half], []))
    names.append(sum(back[half:], []))
    chunks = [spread(chunk(i, part_names), i % 2 == 1) for i, part_names in enumerate(names)]

    def matrices(level, wanted):
        numbers = {where[name, level][0] for name in wanted}
        (number,) = numbers
        return chunks[number], {name: where[name, level][1] for name in wanted}

    full = (plan.parts, plan.kept, plan.groups, plan.rows, plan.width)
    count = len(plan.blocks)
    halves = plan.update_rows // plan.width
    tall = plan.group_rows // plan.rows
    slab_bytes = plan.slab[0] * plan.slab[1] * 2
    one_pass = 2 * plan.targets * plan.sources * plan.groups * LANES

    forward_out, sent, start, arrived, more = [], [], None, [], None
    for level in range(levels):
        last, fresh = level == top, level == 0
        wanted = ["fwd"] + (["rhs"] if fresh else []) + (["inv"] if last else ["upd"])
        blocks, part_of = matrices(level, wanted)
        args, specs = [], []
        if not last:
            args.append(keys[level])
            specs.append(VM)
        if not fresh:
            args += [start] + arrived
            specs += [VM] * (1 + owners)
        if more is not None and not last:
            args.append(more)
            specs.append(VM)
        args += blocks
        specs += [ANY] * count
        outs = [(plan.slab, F32)]
        if last:
            outs.append((plan.slab, BF))
        else:
            outs.append(((plan.slab[0], plan.update_rows), BF))
            outs += [(plan.slab, F32)] + [(plan.slab, BF)] * (owners - 1)
        scratch = [pltpu.VMEM(full, BF)] * (2 if fresh else 1)
        scratch.append(pltpu.VMEM(full if last else (halves,) + full, BF))
        scratch.append(pltpu.SemaphoreType.DMA((count * (2 + halves),)))
        got = call(
            functools.partial(
                forward_kernel, plan, level, part_of, fresh, more is not None and not last
            ),
            args, specs, outs, scratch, one_pass, 24 * slab_bytes,
        )
        forward_out.append(got[0])
        if last:
            solved = got[1]
            break
        sent.append(got[1])
        arrived = [got[2]] + [over_leaf(got[2 + d], d * plan.parts) for d in range(1, owners)]
        ahead_blocks, ahead_part = matrices(level + 1, ["rhs"])
        ahead = level + 1
        is_far = ahead < top
        args = (sent[:ahead] if is_far else []) + ([keys[i] for i in range(ahead)] if is_far else [])
        outs = [(plan.slab, F32)] + ([((owners,) + plan.slab, F32)] if is_far else [])
        got = call(
            functools.partial(ahead_kernel, plan, ahead, ahead_part),
            args + ahead_blocks, [VM] * len(args) + [ANY] * count, outs,
            [pltpu.VMEM(full, BF), pltpu.SemaphoreType.DMA((count,))],
            one_pass * max(1, len(args) // 2), 16 * slab_bytes,
        )
        start, more = got[0], got[1] if is_far else None

    solutions = {top: solved}
    everywhere = {}
    for level in reversed(range(top)):
        above = solutions[level + 1]
        everywhere[level + 1] = [above] + [over_leaf(above, d * plan.parts) for d in range(1, owners)]
        froms = list(range(level + 2, levels))
        known = []
        if froms:
            slabs = sum([everywhere[f] for f in froms], [])
            known = call(
                functools.partial(known_kernel, plan, froms),
                [keys[level]] + slabs, [VM] * (1 + len(slabs)),
                [((plan.groups, plan.chunk, plan.sources), BF)], [],
                one_pass * len(froms), 16 * slab_bytes,
            )
        blocks, part_of = matrices(level, ["upper", "inv"])
        args = [keys[level]] + everywhere[level + 1] + list(known) + [forward_out[level]]
        (solutions[level],) = call(
            functools.partial(backward_kernel, plan, level, part_of, bool(froms)),
            args + blocks, [VM] * len(args) + [ANY] * count, [(plan.slab, BF)],
            [
                pltpu.VMEM((plan.parts, plan.kept, plan.groups, plan.group_rows, plan.width), BF),
                pltpu.VMEM(full, BF),
                pltpu.SemaphoreType.DMA((count * (1 + tall),)),
            ],
            one_pass, 24 * slab_bytes,
        )

    piece = (levels, plan.kept * plan.chunk, LANES)
    own = call(
        functools.partial(pieces_kernel, plan),
        [solutions[level] for level in range(levels)], [VM] * levels,
        [(piece, BF)] * count, [], 1, 8 * slab_bytes,
    )
    both = ("leaf", "grid")

    def swap(x, dp, dg):
        if (dp, dg) == (0, 0):
            return x
        g = plan.groups
        moves = [(i, ((i // g) ^ dp) * g + ((i % g) ^ dg)) for i in range(plan.leaves * g)]
        return lax.ppermute(x, both, moves)

    theirs = [swap(x, dp, dg) for x, (dp, dg) in zip(own, plan.blocks)]
    (result,) = call(
        functools.partial(result_kernel, plan),
        theirs, [VM] * count, [(rhs.shape, BF)],
        [pltpu.VMEM((levels, plan.kept, plan.columns, LANES), BF)], 1, 8 * slab_bytes,
    )
    return result


def solution(mesh):
    def local(rhs, fwd_inv, bwd_inv, upd_t, bwd_t, dest_owner, dest_row):
        plan = Plan(mesh, rhs, upd_t, bwd_t)
        return solve(plan, rhs, fwd_inv, bwd_inv, upd_t, bwd_t, dest_owner, dest_row)

    rows = P(None, "leaf", "grid", None)
    placed = (rows, rows, rows, rows, rows, P(None, "leaf", "grid", None, None), rows)
    return jax.shard_map(local, mesh=mesh, in_specs=placed, out_specs=rows, check_vma=False)
```

```python
import functools

import jax
import jax.numpy as jnp
from jax import lax
from jax.experimental import pallas as pl
from jax.experimental.pallas import tpu as pltpu
from jax.sharding import PartitionSpec as P

BF = jnp.bfloat16
F32 = jnp.float32
LANES = 128
ROWS_AT_ONCE = 256
VMEM_BYTES = 16 * 1024 * 1024
PACK_VMEM_BYTES = 60 * 1024 * 1024


def nn(a, b):
    return lax.dot_general(a, b, (((1,), (0,)), ((), ())), preferred_element_type=F32)


def nt(a, b):
    return lax.dot_general(a, b, (((1,), (1,)), ((), ())), preferred_element_type=F32)


class Plan:
    def __init__(self, mesh, rhs, upd_t, bwd_t):
        self.levels, self.kept, self.rows, self.columns = rhs.shape
        self.leaves, self.groups = mesh.shape["leaf"], mesh.shape["grid"]
        self.parts = 2 if self.leaves % 2 == 0 else 1
        self.owners = self.leaves // self.parts
        self.supers = self.parts * self.kept
        self.chunk = self.columns // (self.groups * self.parts)
        self.width = self.rows * self.groups
        self.update_rows = upd_t.shape[3]
        self.group_rows = bwd_t.shape[2]
        self.slab = (self.supers * self.chunk, self.width)
        self.chips = [(dp, dg) for dg in range(0, self.groups, 2) for dp in range(self.parts)]
        self.coded = -(-3 * (self.levels - 1) // 16) * 16
        self.sources = self.supers * self.group_rows
        self.blocks = [(dp, dg) for dp in range(self.parts) for dg in range(self.groups)]

    def place(self):
        leaf, grid = lax.axis_index("leaf"), lax.axis_index("grid")
        return leaf // self.parts, leaf % self.parts, grid


def fetch(plan, blocks, pieces, sems):
    _, part, grid = plan.place()
    copies, k = [], plan.kept
    for slab, make in pieces:
        group = []
        for ref, (dp, dg) in zip(blocks, plan.blocks):
            sem = sems.at[len(copies) * len(plan.blocks) + len(group)]
            source = ref.at[pl.ds(slab * k, k)]
            group.append(pltpu.make_async_copy(source, make(part ^ dp, grid ^ dg), sem))
            group[-1].start()
        copies.append(group)
    return copies


def wait(group):
    for copy in group:
        copy.wait()


def matrix(plan, ref, s):
    whole = ref[s // plan.kept, s % plan.kept]
    return whole.reshape(-1, whole.shape[-1])


def joined(plan, stacks, slab, s, count=1):
    own, other = stacks
    first = lax.axis_index("grid") % 2 == 0
    rows = []
    for x in range(plan.groups // 2):
        at = [(x, s // plan.kept, (slab + i) * plan.kept + s % plan.kept) for i in range(count)]
        rows += [jnp.where(first, own[i], other[i]) for i in at]
        rows += [jnp.where(first, other[i], own[i]) for i in at]
    return jnp.concatenate(rows, axis=0)


def start_slab(plan, pieces, at, upper):
    out = []
    for pair in range(plan.groups // 2):
        out.append(
            jnp.concatenate(
                [
                    cross(*[pieces[p, 2 * pair + i, at].astype(F32) for i in range(2)])[upper]
                    for p in range(plan.parts)
                ],
                axis=0,
            )
        )
    return jnp.concatenate(out, axis=1)


def fetch_pieces(plan, blocks, first, count, target, sems, at):
    _, part, grid = plan.place()
    lanes = pl.ds(pl.multiple_of(grid % 2 * LANES, LANES), LANES)
    copies = []
    for ref, (dp, dg) in zip(blocks, plan.blocks):
        for i in range(count):
            copy = pltpu.make_async_copy(
                ref.at[first + i, :, lanes],
                target.at[part ^ dp, grid ^ dg, i],
                sems.at[at + len(copies)],
            )
            copy.start()
            copies.append(copy)
    return copies


def copy_matrices(plan, sources, layout, target, sems, at):
    copies = []
    for i, (source, index) in enumerate(layout):
        to = target.at[pl.ds(i * plan.kept, plan.kept)]
        copies.append(pltpu.make_async_copy(sources[source].at[index], to, sems.at[at + i]))
        copies[-1].start()
    return copies


def pack_kernel(plan, layouts, *refs):
    sources, targets, sems = refs[:4], refs[-1 - len(layouts) : -1], refs[-1]
    copies = []
    for layout, target in zip(layouts, targets):
        copies += copy_matrices(plan, sources, layout, target, sems, len(copies))
    wait(copies)


def first_kernel(plan, layout, second, pairs, *refs):
    refs = list(refs)
    sources = [refs.pop(0) for _ in range(4)]
    rhs_ref, owner_ref, row_ref = [refs.pop(0) for _ in range(3)]
    firsts, second_ref = [refs.pop(0) for _ in plan.chips], refs.pop(0)
    raw_ref, turned_ref, sent_ref, sems = refs
    owner_at, part, grid = plan.place()
    k, r, c = plan.kept, plan.rows, plan.chunk
    fill = pltpu.make_async_copy(rhs_ref, raw_ref, sems.at[0])
    fill.start()
    copies = []
    for target in firsts:
        copies += copy_matrices(plan, sources, layout, target, sems, 1 + len(copies))
    copies += copy_matrices(plan, sources, second, second_ref, sems, 1 + len(copies))
    first = len(layout) * k
    leaf_to, row_to = [
        jnp.concatenate([ref[level, 0] for level in range(plan.levels - 1)], axis=0) for ref in (owner_ref, row_ref)
    ]
    block_to = row_to // r
    super_to = (block_to // k * plan.parts + leaf_to % plan.parts) * k + block_to % k
    fields = [(leaf_to // plan.parts) ^ owner_at, row_to % r, super_to]
    lines = [x[i : i + 1].astype(F32) for i in range(plan.levels - 1) for x in fields]
    lines.append(jnp.zeros((r - len(lines), plan.width), F32))
    shape = (plan.width, plan.width)
    now, then = lax.broadcasted_iota(jnp.int32, shape, 0), lax.broadcasted_iota(jnp.int32, shape, 1)
    move = jnp.where(now == then % plan.group_rows * k + then // plan.group_rows, 1.0, 0.0).astype(BF)
    lines = nn(jnp.concatenate(lines, axis=0).astype(BF), move).astype(BF)
    for i in range(len(plan.chips)):
        sent_ref[i, len(pairs)] = lines
    shape = (plan.columns, plan.columns)
    same = lax.broadcasted_iota(jnp.int32, shape, 0) == lax.broadcasted_iota(jnp.int32, shape, 1)
    same = jnp.where(same, 1.0, 0.0).astype(BF)
    fill.wait()
    for j, pair in enumerate(pairs):
        for s in range(k):
            two = [raw_ref[level, s] for level in pair]
            two += [jnp.zeros((r, plan.columns), BF)] * (2 - len(two))
            turned_ref[s] = nt(same, jnp.concatenate(two, axis=0)).astype(BF)
        for i, (dp, dg) in enumerate(plan.chips):
            for s in range(k):
                for core in range(2):
                    column = ((part ^ dp) * plan.groups + (grid ^ dg) // 2 * 2 + core) * c
                    piece = turned_ref[s, pl.ds(pl.multiple_of(column, c), c), :]
                    sent_ref[i, j, s * c : (s + 1) * c, core * LANES : (core + 1) * LANES] = piece
    extra = len(pairs) + 1
    for i, target in enumerate(firsts):
        copy = pltpu.make_async_copy(sent_ref.at[i], target.at[pl.ds(first, extra)], sems.at[1 + len(copies)])
        copy.start()
        copies.append(copy)
    wait(copies)


def onehot(keys, first, rows):
    iota = lax.broadcasted_iota(jnp.int32, (rows, keys.shape[1]), 0)
    return jnp.where(iota == keys - first, 1.0, 0.0).astype(BF)


def cross(even, odd):
    half = even.shape[1] // 2
    low = lax.broadcasted_iota(jnp.int32, even.shape, 1) < half
    return (
        jnp.where(low, even, pltpu.roll(odd, half, 1)),
        jnp.where(low, pltpu.roll(even, half, 1), odd),
    )


def owners_at_once(plan):
    return min(plan.owners, max(2, ROWS_AT_ONCE // plan.rows))


def scatter(plan, sent, key_ref, level, levels_to, emit):
    c, per = plan.chunk, owners_at_once(plan)
    for pair in range(plan.groups // 2):
        given = []
        for g in (2 * pair, 2 * pair + 1):
            lanes = slice(g * plan.group_rows, (g + 1) * plan.group_rows)
            whole = jnp.concatenate([sent[s * c : (s + 1) * c, lanes] for s in range(plan.supers)], axis=1)
            super_to = key_ref[1, level, g : g + 1, :]
            given.append(
                jnp.concatenate(
                    [
                        whole * jnp.where(super_to == to * plan.supers + s, 1.0, 0.0).astype(BF)
                        for to in levels_to
                        for s in range(plan.supers)
                    ],
                    axis=0,
                )
            )
        for first in range(0, plan.owners, per):
            even, odd = [
                nt(
                    given[i],
                    onehot(
                        key_ref[0, level, 2 * pair + i : 2 * pair + i + 1, :],
                        first * plan.rows,
                        per * plan.rows,
                    ),
                )
                for i in range(2)
            ]
            for j in range(0, per, 2):
                at = slice(j * plan.rows, (j + 2) * plan.rows)
                one, two = cross(even[:, at], odd[:, at])
                for i, to in enumerate(levels_to):
                    rows = slice(i * plan.slab[0], (i + 1) * plan.slab[0])
                    emit(to, first + j, pair, one[rows])
                    emit(to, first + j + 1, pair, two[rows])


def gather(plan, froms, key_ref, level, done):
    c, per = plan.chunk, owners_at_once(plan)
    for pair in range(plan.groups // 2):
        lanes = slice(pair * LANES, (pair + 1) * LANES)
        total = [None, None]
        for first in range(0, plan.owners, per):
            given = [[], []]
            for _, slabs in froms:
                got = [[], []]
                for d in range(first, first + per, 2):
                    halves = cross(slabs[d][:, lanes].astype(F32), slabs[d + 1][:, lanes].astype(F32))
                    for i in range(2):
                        got[i].append(halves[i])
                for i in range(2):
                    given[i].append(jnp.concatenate(got[i], axis=1).astype(BF))
            for i in range(2):
                g = 2 * pair + i
                keys = key_ref[0, level, g : g + 1, :]
                super_to = key_ref[1, level, g : g + 1, :]
                found = nn(
                    jnp.concatenate(given[i], axis=0), onehot(keys, first * plan.rows, per * plan.rows)
                )
                at = 0
                for level_from, _ in froms:
                    for s in range(plan.supers):
                        term = jnp.where(super_to == level_from * plan.supers + s, found[at : at + c], 0.0)
                        total[i] = term if total[i] is None else total[i] + term
                        at += c
        for i in range(2):
            done(2 * pair + i, total[i])


def gate_kernel(*refs):
    pass


def stack_kernel(plan, counts, *refs):
    _, part, grid = plan.place()
    refs = list(refs)
    given = [[(refs.pop(0), first) for first in firsts] for firsts in counts]
    for parts, out in zip(given, refs[len(refs) - len(counts) :]):
        for i, (ref, first) in enumerate(parts):
            if len(out.shape) > 4 and len(ref.shape) > 3:
                out[(grid // 2) ^ i] = ref[...]
            elif len(out.shape) > 4:
                out[(grid // 2) ^ (i // plan.parts), part ^ (i % plan.parts)] = ref[...]
            else:
                out[part ^ i] = ref[first : first + out.shape[1]]


def forward_kernel(plan, level, part_of, added, *refs):
    refs = list(refs)
    last, fresh = level == plan.levels - 1, level == 0
    c, halves = plan.chunk, plan.update_rows // plan.width
    key_ref = None if last or fresh else refs.pop(0)
    if not fresh:
        start_ref, *arrived = [refs.pop(0) for _ in range(1 + plan.owners)]
    more_ref = refs.pop(0) if added else None
    blocks = [refs.pop(0) for _ in (plan.blocks if fresh else range(2))]
    if fresh:
        del refs[: len(plan.chips)]
    out_ref = refs.pop(0)
    if last:
        solved_ref = refs.pop(0)
    else:
        sent_ref = refs.pop(0)
        slab_refs = [refs.pop(0) for _ in range(plan.owners)]
    if fresh:
        key_ref = refs.pop(0)
        next_refs = [refs.pop(0) for _ in range(plan.levels - 1)]
        coded_ref, piece_ref, inv_ref, upd_ref, sems = refs
        _, part, grid = plan.place()
        pairs, size = piece_ref.shape[2], len(plan.blocks)
        first = blocks[0].shape[0] - 1 - pairs
        arriving = fetch_pieces(plan, blocks, first, pairs, piece_ref, sems, size * (2 + halves))
        pieces = [(part_of["fwd"], lambda p, g: inv_ref.at[p, :, g])]
        for half in range(halves):
            pieces.append((part_of["upd"] + half, lambda p, g, half=half: upd_ref.at[half, p, :, g]))
        copies = fetch(plan, blocks, pieces, sems)
        coded = []
        for i, (ref, (dp, dg)) in enumerate(zip(blocks, plan.blocks)):
            coded.append(
                pltpu.make_async_copy(
                    ref.at[ref.shape[0] - 1, pl.ds(0, plan.coded)],
                    coded_ref.at[part ^ dp, grid ^ dg],
                    sems.at[(1 + halves) * size + i],
                )
            )
            coded[-1].start()
        wait(arriving)
        block = start_slab(plan, piece_ref, 0, 0)
        wait(copies[0])
        lower = lambda s: matrix(plan, inv_ref, s)
        update = lambda s, half: matrix(plan, upd_ref.at[half], s)
    else:
        block = start_ref[...] - arrived[0][...]
        for ref in arrived[1:]:
            block = block - ref[...].astype(F32)
        lower = lambda s: joined(plan, blocks, part_of["fwd"], s)
        update = lambda s, half: joined(plan, blocks, part_of["upd"] + half, s)
    block = block.astype(BF)
    solved = jnp.concatenate(
        [nt(block[s * c : (s + 1) * c], lower(s)) for s in range(plan.supers)], axis=0
    )
    out_ref[...] = solved
    lowered = solved.astype(BF)
    if last:
        for s in range(plan.supers):
            at = slice(s * c, (s + 1) * c)
            solved_ref[at, :] = nt(lowered[at], joined(plan, blocks, part_of["inv"], s)).astype(BF)
        return
    if fresh:
        wait(coded)
        for to in range(plan.levels - 1):
            for g in range(plan.groups):
                distance, row, super_to = [
                    jnp.concatenate(
                        [coded_ref[p, g, 3 * to + i : 3 * to + i + 1, :] for p in range(plan.parts)], axis=1
                    ).astype(F32)
                    for i in range(3)
                ]
                key_ref[0, to, g : g + 1, :] = (distance * plan.rows + row).astype(jnp.int32)
                key_ref[1, to, g : g + 1, :] = super_to.astype(jnp.int32)
        for group in copies[1:]:
            wait(group)
    for s in range(plan.supers):
        at = slice(s * c, (s + 1) * c)
        for half in range(halves):
            lanes = slice(half * plan.width, (half + 1) * plan.width)
            sent_ref[at, lanes] = nn(lowered[at], update(s, half)).astype(BF)

    def emit(to, distance, pair, value):
        lanes = slice(pair * LANES, (pair + 1) * LANES)
        if more_ref is not None:
            value = value + more_ref[distance, :, lanes]
        slab_refs[distance][:, lanes] = value.astype(slab_refs[distance].dtype)

    scatter(plan, sent_ref[...], key_ref, level, [level + 1], emit)
    if fresh:
        for i, ref in enumerate(next_refs):
            ref[...] = start_slab(plan, piece_ref, (i + 1) // 2, (i + 1) % 2)


def ahead_kernel(plan, level, *refs):
    sent, key_ref, more_ref = refs[:level], refs[level], refs[level + 1]
    for i, ref in enumerate(sent):

        def emit(to, distance, pair, value, first=i == 0):
            lanes = slice(pair * LANES, (pair + 1) * LANES)
            if not first:
                value = value + more_ref[distance, :, lanes]
            more_ref[distance, :, lanes] = value

        scatter(plan, ref[...], key_ref, i, [level + 1], emit)


def known_kernel(plan, level, froms, *refs):
    key_ref, out_ref = refs[0], refs[-1]
    slabs = [refs[1 + i * plan.owners : 1 + (i + 1) * plan.owners] for i in range(len(froms))]

    def done(g, value):
        out_ref[g] = value.astype(BF)

    gather(plan, list(zip(froms, slabs)), key_ref, level, done)


def backward_kernel(plan, level, part_of, known, *refs):
    refs = list(refs)
    key_ref = refs.pop(0)
    slabs = [refs.pop(0) for _ in range(plan.owners)]
    known_ref = refs.pop(0) if known else None
    forward_ref, *blocks, solved_ref = refs
    c, tall = plan.chunk, plan.group_rows // plan.rows
    pulled = [None] * plan.groups

    def done(g, value):
        if known:
            value = value + known_ref[g].astype(F32)
        pulled[g] = value.astype(BF)

    gather(plan, [(level + 1, slabs)], key_ref, level, done)
    for s in range(plan.supers):
        at = slice(s * c, (s + 1) * c)
        lanes = slice(s * plan.group_rows, (s + 1) * plan.group_rows)
        whole = jnp.concatenate([p[:, lanes] for p in pulled], axis=1)
        upper = nn(whole, joined(plan, blocks, part_of["upper"], s, tall))
        reduced = (forward_ref[at, :] - upper).astype(BF)
        solved_ref[at, :] = nt(reduced, joined(plan, blocks, part_of["inv"], s)).astype(BF)


def pieces_kernel(plan, *refs):
    _, part, grid = plan.place()
    slabs, outs = refs[: plan.levels], refs[plan.levels :]
    rows, half = plan.kept * plan.chunk, plan.rows
    low = lax.broadcasted_iota(jnp.int32, (rows, LANES), 1) < half
    for out, (dp, dg) in zip(outs, plan.blocks):
        first = pl.multiple_of((part ^ dp) * rows, rows)
        lane = pl.multiple_of((grid ^ dg) * half // LANES * LANES, LANES)
        turn = (grid ^ dg) * half % LANES
        for i in range(0, plan.levels, 2):
            two = [slab[pl.ds(first, rows), pl.ds(lane, LANES)].astype(F32) for slab in slabs[i : i + 2]]
            one = pltpu.roll(two[0], turn, 1)
            if len(two) > 1:
                one = jnp.where(low, one, pltpu.roll(two[1], half - turn, 1))
            out[i // 2] = one.astype(BF)


def result_kernel(plan, *refs):
    _, part, grid = plan.place()
    refs = list(refs)
    scratch, out = refs.pop(), refs.pop()
    c = plan.chunk
    shape = (plan.rows, LANES)
    lane = lax.broadcasted_iota(jnp.int32, shape, 1)
    row = lax.broadcasted_iota(jnp.int32, shape, 0)
    picks = [jnp.where(lane == row + i * plan.rows, 1.0, 0.0).astype(BF) for i in range(2)]
    for k in range(plan.kept):
        for ref, (dp, dg) in zip(refs, plan.blocks):
            at = ((part ^ dp) * plan.groups + (grid ^ dg)) * c
            for i in range((plan.levels + 1) // 2):
                scratch[i, k, pl.ds(pl.multiple_of(at, c), c), :] = ref[i, k * c : (k + 1) * c, :]
    for level in range(plan.levels):
        for k in range(plan.kept):
            out[level, k] = nt(picks[level % 2], scratch[level // 2, k]).astype(BF)


VM = pl.BlockSpec(memory_space=pltpu.VMEM)
ANY = pl.BlockSpec(memory_space=pltpu.HBM)
UNREAD = pl.BlockSpec(memory_space=pl.ANY)


def call(body, args, specs, outs, scratch, flops, moved, vmem=VMEM_BYTES):
    return pl.pallas_call(
        body,
        in_specs=specs,
        out_specs=[VM] * len(outs),
        out_shape=[jax.ShapeDtypeStruct(shape, dtype) for shape, dtype in outs],
        scratch_shapes=scratch,
        compiler_params=pltpu.CompilerParams(vmem_limit_bytes=vmem),
        cost_estimate=pl.CostEstimate(flops=flops, bytes_accessed=moved, transcendentals=0),
    )(*args)


def gate(x, *others):
    return pl.pallas_call(
        gate_kernel,
        in_specs=[UNREAD] * (1 + len(others)),
        out_specs=UNREAD,
        out_shape=jax.ShapeDtypeStruct(x.shape, x.dtype),
        input_output_aliases={0: 0},
        compiler_params=pltpu.CompilerParams(vmem_limit_bytes=2**20),
        cost_estimate=pl.CostEstimate(flops=0, bytes_accessed=0, transcendentals=0),
    )(x, *others)


def stack(plan, jobs, *others):
    args = [x for parts, _ in jobs for x, _ in parts]
    return call(
        functools.partial(stack_kernel, plan, [[first for _, first in parts] for parts, _ in jobs]),
        args + list(others), [VM] * len(args) + [UNREAD] * len(others),
        [(shape, BF) for _, shape in jobs], [], 1, 2**19,
    )


def solve(plan, rhs, fwd_inv, bwd_inv, upd_t, bwd_t, dest_owner, dest_row):
    levels, owners = plan.levels, plan.owners
    owner_at, part, grid = plan.place()

    def over_leaf(x, step):
        return lax.ppermute(x, "leaf", [(i, i ^ step) for i in range(plan.leaves)])

    def over_grid(x, step):
        return lax.ppermute(x, "grid", [(i, i ^ step) for i in range(plan.groups)])

    def swap(x, dp, dg):
        if (dp, dg) == (0, 0):
            return x
        g = plan.groups
        moves = [(i, ((i // g) ^ dp) * g + ((i % g) ^ dg)) for i in range(plan.leaves * g)]
        return lax.ppermute(x, ("leaf", "grid"), moves)

    top, every = levels - 1, slice(None)
    halves = plan.update_rows // plan.width
    tall = plan.group_rows // plan.rows

    def parts_of(name, level):
        if name == "upd":
            return [(2, (level, every, every, pl.ds(h * plan.width, plan.width))) for h in range(halves)]
        if name == "upper":
            return [(3, (level, every, pl.ds(h * plan.rows, plan.rows))) for h in range(tall)]
        return [(dict(fwd=0, inv=1)[name], (level,))]

    names = [[("fwd", level), ("upd", level)] for level in range(top)]
    names.append([("fwd", top), ("inv", top)])
    names += [[("upper", level), ("inv", level)] for level in reversed(range(top))]
    where, layouts = {}, []
    for number, chunk in enumerate(names):
        layouts.append([])
        for name, level in chunk:
            where[name, level] = (number, len(layouts[-1]))
            layouts[-1] += parts_of(name, level)
    pairs = [tuple(range(i, min(i + 2, levels))) for i in range(0, levels, 2)]
    slab = (plan.rows, plan.width)
    matrices_given = (fwd_inv, bwd_inv, upd_t, bwd_t)

    ways, extra = len(plan.chips), len(pairs) + 1
    *given, second = call(
        functools.partial(first_kernel, plan, layouts[0], layouts[1], pairs),
        [*matrices_given, rhs, dest_owner.reshape(dest_row.shape), dest_row],
        [ANY] * 5 + [VM] * 2,
        [((len(layouts[0]) * plan.kept + extra,) + slab, BF)] * ways
        + [((len(layouts[1]) * plan.kept,) + slab, BF)],
        [
            pltpu.VMEM(rhs.shape, BF),
            pltpu.VMEM((plan.kept, plan.columns, LANES), BF),
            pltpu.VMEM((ways, extra) + slab, BF),
            pltpu.SemaphoreType.DMA((1 + ways * (len(layouts[0]) + 1) + len(layouts[1]),)),
        ],
        1, 2**20, PACK_VMEM_BYTES,
    )
    sizes = [len(x) * plan.kept for x in layouts]
    later = levels + 1
    grouped = [layouts[2], sum(layouts[3:later], []), sum(layouts[later:], [])]
    owned = call(
        functools.partial(pack_kernel, plan, grouped),
        [*matrices_given, given[0]], [ANY] * 4 + [UNREAD],
        [((len(x) * plan.kept,) + slab, BF) for x in grouped],
        [pltpu.SemaphoreType.DMA((sum(len(x) for x in grouped),))],
        1, 2**20,
    )
    given[-1] = gate(given[-1], owned[0])
    got = {chip: swap(x, *chip) for chip, x in zip(plan.chips, given)}
    chunks = {0: [got[dp, dg] if dg % 2 == 0 else over_grid(got[dp, dg - 1], 1) for dp, dg in plan.blocks]}

    def to_part(x):
        return [x] + [over_leaf(x, dp) for dp in range(1, plan.parts)]

    def to_chip(x):
        return [x] + [over_grid(x, dg) for dg in range(2, plan.groups, 2)]

    chip_there = got[plan.chips[-2]]
    second = to_part(gate(second, chip_there))
    second = second + sum([[over_grid(x, dg) for x in second] for dg in range(2, plan.groups, 2)], [])
    from_part, two = {}, {1: [(x, 0) for x in second]}

    def slices(first, last, x):
        parts, at = to_part(x), 0
        for number in range(first, last):
            from_part[number] = [(part, at) for part in parts]
            at += sizes[number]
        return parts[-1]

    marks = [slices(2, 3, gate(owned[0], chip_there))]
    before_first = second[1:] + marks

    def advance(stage, mark):
        if stage == 0:
            marks.append(slices(3, later, gate(owned[1], mark)))
        if stage == 1:
            slices(later, len(layouts), gate(owned[2], mark, marks[-1]))
        jobs, done = [], []
        if stage + 1 in two:
            shape = (plan.groups // 2, plan.parts, sizes[stage + 1]) + slab
            jobs.append((two[stage + 1], shape))
            done.append(stage + 1)
        if stage + 2 in from_part:
            jobs.append((from_part[stage + 2], (plan.parts, sizes[stage + 2]) + slab))
            done.append(stage + 2)
        for x, number in zip(stack(plan, jobs, mark) if jobs else [], done):
            if number == stage + 1:
                chunks[number] = [x, over_grid(x, 1)]
            else:
                two[number] = [(x, 0) for x in to_chip(x)]

    def matrices(level, wanted):
        (number,) = {where[name, level][0] for name in wanted}
        return chunks[number], {name: where[name, level][1] for name in wanted}

    full = (plan.parts, plan.kept, plan.groups, plan.rows, plan.width)
    slab_bytes = plan.slab[0] * plan.slab[1] * 2
    one_pass = 2 * plan.slab[0] * plan.slab[1] * plan.sources * plan.groups * max(1, owners // 4)

    forward_out, sent, starts, arrived, more = [], [], {}, [], None
    for level in range(levels):
        last, fresh = level == top, level == 0
        blocks, part_of = matrices(level, ["fwd", "inv" if last else "upd"])
        count = len(blocks)
        args, specs = [], []
        if not last and not fresh:
            args.append(keys)
            specs.append(VM)
        if not fresh:
            args += [starts[level]] + arrived
            specs += [VM] * (1 + owners)
        if more is not None and not last:
            args.append(more)
            specs.append(VM)
        args += blocks
        specs += [ANY if fresh else VM] * count
        if fresh:
            args += before_first
            specs += [UNREAD] * len(before_first)
        outs = [(plan.slab, F32)]
        if last:
            outs.append((plan.slab, BF))
        else:
            outs.append(((plan.slab[0], plan.update_rows), BF))
            outs += [(plan.slab, F32)] + [(plan.slab, BF)] * (owners - 1)
        if fresh:
            outs.append(((2, levels - 1, plan.groups, plan.sources), jnp.int32))
            outs += [(plan.slab, F32)] * top
        scratch = []
        if fresh:
            scratch = [
                pltpu.VMEM((plan.parts, plan.groups, plan.coded, plan.width), BF),
                pltpu.VMEM((plan.parts, plan.groups, len(pairs), plan.rows, LANES), BF),
                pltpu.VMEM(full, BF),
                pltpu.VMEM((halves,) + full, BF),
                pltpu.SemaphoreType.DMA((len(plan.blocks) * (2 + halves + len(pairs)),)),
            ]
        got = call(
            functools.partial(
                forward_kernel, plan, level, part_of, more is not None and not last
            ),
            args, specs, outs, scratch, one_pass, 24 * slab_bytes,
        )
        forward_out.append(got[0])
        if last:
            solved = got[1]
            break
        sent.append(got[1])
        if fresh:
            keys = got[-1 - top]
            starts.update(zip(range(1, levels), got[-top:]))
        arrived = [got[2]] + [over_leaf(got[2 + d], d * plan.parts) for d in range(1, owners)]
        advance(level, got[1])
        more = None
        if level + 1 < top:
            (more,) = call(
                functools.partial(ahead_kernel, plan, level + 1),
                sent + [keys], [VM] * (len(sent) + 1), [((owners,) + plan.slab, F32)], [],
                one_pass * len(sent), 16 * slab_bytes,
            )

    solutions = {top: solved}
    everywhere = {}
    for level in reversed(range(top)):
        above = solutions[level + 1]
        everywhere[level + 1] = [above] + [over_leaf(above, d * plan.parts) for d in range(1, owners)]
        froms = list(range(level + 2, levels))
        known = []
        if froms:
            slabs = sum([everywhere[f] for f in froms], [])
            known = call(
                functools.partial(known_kernel, plan, level, froms),
                [keys] + slabs, [VM] * (1 + len(slabs)),
                [((plan.groups, plan.chunk, plan.sources), BF)], [],
                one_pass * len(froms), 16 * slab_bytes,
            )
        advance(levels + top - level - 2, above)
        blocks, part_of = matrices(level, ["upper", "inv"])
        args = [keys] + everywhere[level + 1] + list(known) + [forward_out[level]]
        (solutions[level],) = call(
            functools.partial(backward_kernel, plan, level, part_of, bool(froms)),
            args + blocks, [VM] * (len(args) + len(blocks)), [(plan.slab, BF)], [],
            one_pass, 24 * slab_bytes,
        )

    piece = ((levels + 1) // 2, plan.kept * plan.chunk, LANES)
    own = call(
        functools.partial(pieces_kernel, plan),
        [solutions[level] for level in range(levels)], [VM] * levels,
        [(piece, BF)] * len(plan.blocks), [], 1, 8 * slab_bytes,
    )
    theirs = [swap(x, dp, dg) for x, (dp, dg) in zip(own, plan.blocks)]
    (result,) = call(
        functools.partial(result_kernel, plan),
        theirs, [VM] * len(theirs), [(rhs.shape, BF)],
        [pltpu.VMEM(((levels + 1) // 2, plan.kept, plan.columns, LANES), BF)], 1, 8 * slab_bytes,
    )
    return result


def solution(mesh):
    def local(rhs, fwd_inv, bwd_inv, upd_t, bwd_t, dest_owner, dest_row):
        plan = Plan(mesh, rhs, upd_t, bwd_t)
        return solve(plan, rhs, fwd_inv, bwd_inv, upd_t, bwd_t, dest_owner, dest_row)

    rows = P(None, "leaf", "grid", None)
    placed = (rows, rows, rows, rows, rows, P(None, "leaf", "grid", None, None), rows)
    return jax.shard_map(local, mesh=mesh, in_specs=placed, out_specs=rows, check_vma=False)
```

```python
import functools

import jax
import jax.numpy as jnp
from jax import lax
from jax.experimental import pallas as pl
from jax.experimental.pallas import tpu as pltpu
from jax.sharding import PartitionSpec as P

BF = jnp.bfloat16
F32 = jnp.float32
LANES = 128
ROWS_AT_ONCE = 256
VMEM_BYTES = 16 * 1024 * 1024
PACK_VMEM_BYTES = 60 * 1024 * 1024


def nn(a, b):
    return lax.dot_general(a, b, (((1,), (0,)), ((), ())), preferred_element_type=F32)


def nt(a, b):
    return lax.dot_general(a, b, (((1,), (1,)), ((), ())), preferred_element_type=F32)


class Plan:
    def __init__(self, mesh, rhs, upd_t, bwd_t):
        self.levels, self.kept, self.rows, self.columns = rhs.shape
        self.leaves, self.groups = mesh.shape["leaf"], mesh.shape["grid"]
        self.parts = 2 if self.leaves % 2 == 0 else 1
        self.owners = self.leaves // self.parts
        self.supers = self.parts * self.kept
        self.chunk = self.columns // (self.groups * self.parts)
        self.width = self.rows * self.groups
        self.update_rows = upd_t.shape[3]
        self.group_rows = bwd_t.shape[2]
        self.slab = (self.supers * self.chunk, self.width)
        self.chips = [(dp, dg) for dg in range(0, self.groups, 2) for dp in range(self.parts)]
        self.shared = self.levels % 2 == 1
        self.coded = -(-3 * (self.levels - 1) // 16) * 16
        self.sources = self.supers * self.group_rows
        self.blocks = [(dp, dg) for dp in range(self.parts) for dg in range(self.groups)]

    def place(self):
        leaf, grid = lax.axis_index("leaf"), lax.axis_index("grid")
        return leaf // self.parts, leaf % self.parts, grid


def wait(group):
    for copy in group:
        copy.wait()


def block_of(plan, stacks, p, g, row):
    same = lax.axis_index("grid") % 2 == g % 2
    return jnp.where(same, stacks[0][g // 2, p, row], stacks[1][g // 2, p, row])


def joined(plan, stacks, slab, s, count=1):
    p, k = s // plan.kept, s % plan.kept
    rows = [
        block_of(plan, stacks, p, g, (slab + i) * plan.kept + k)
        for g in range(plan.groups)
        for i in range(count)
    ]
    return jnp.concatenate(rows, axis=0)


def start_slab(plan, stacks, first, level):
    low_core = lax.axis_index("grid") % 2 == 0

    def piece(p, g):
        both = block_of(plan, stacks, p, g, first + level // 2).astype(F32)
        return jnp.where(low_core, both[:, :LANES], both[:, LANES:])

    out = []
    for pair in range(plan.groups // 2):
        halves = [cross(piece(p, 2 * pair), piece(p, 2 * pair + 1))[level % 2] for p in range(plan.parts)]
        out.append(jnp.concatenate(halves, axis=0))
    return jnp.concatenate(out, axis=1)


def coded_lines(plan, stacks, p, g, end):
    if not plan.shared:
        return block_of(plan, stacks, p, g, end)[: plan.coded].astype(F32)
    both = block_of(plan, stacks, p, g, end - 1).astype(F32)
    lines = jnp.where(lax.axis_index("grid") % 2 == 0, both[:, :LANES], both[:, LANES:])
    low = lax.broadcasted_iota(jnp.int32, (plan.coded, LANES), 1) < LANES // 2
    out = []
    for i in range(0, 2 * plan.width // LANES, 2):
        one, two = [lines[(i + j) * plan.coded : (i + j + 1) * plan.coded] for j in range(2)]
        out.append(jnp.where(low, pltpu.roll(one, LANES // 2, 1), two))
    return jnp.concatenate(out, axis=1)


def copy_matrices(plan, sources, layout, target, sems, at):
    copies = []
    for i, (source, index) in enumerate(layout):
        to = target.at[pl.ds(i * plan.kept, plan.kept)]
        copies.append(pltpu.make_async_copy(sources[source].at[index], to, sems.at[at + i]))
        copies[-1].start()
    return copies


def pack_kernel(plan, layouts, *refs):
    sources, targets, sems = refs[:4], refs[-1 - len(layouts) : -1], refs[-1]
    copies = []
    for layout, target in zip(layouts, targets):
        copies += copy_matrices(plan, sources, layout, target, sems, len(copies))
    wait(copies)


def first_kernel(plan, layout, second, pairs, *refs):
    refs = list(refs)
    sources = [refs.pop(0) for _ in range(4)]
    rhs_ref, owner_ref, row_ref = [refs.pop(0) for _ in range(3)]
    firsts, second_ref = [refs.pop(0) for _ in plan.chips], refs.pop(0)
    raw_ref, turned_ref, sems = refs
    owner_at, part, grid = plan.place()
    k, r, c = plan.kept, plan.rows, plan.chunk
    fill = pltpu.make_async_copy(rhs_ref, raw_ref, sems.at[0])
    fill.start()
    copies = []
    for target in firsts:
        copies += copy_matrices(plan, sources, layout, target, sems, 1 + len(copies))
    copies += copy_matrices(plan, sources, second, second_ref, sems, 1 + len(copies))
    first = len(layout) * k
    leaf_to, row_to = [
        jnp.concatenate([ref[level, 0] for level in range(plan.levels - 1)], axis=0) for ref in (owner_ref, row_ref)
    ]
    block_to = row_to // r
    super_to = (block_to // k * plan.parts + leaf_to % plan.parts) * k + block_to % k
    fields = [(leaf_to // plan.parts) ^ owner_at, row_to % r, super_to]
    lines = [x[i : i + 1].astype(F32) for i in range(plan.levels - 1) for x in fields]
    lines.append(jnp.zeros((r - len(lines), plan.width), F32))
    shape = (plan.width, plan.width)
    now, then = lax.broadcasted_iota(jnp.int32, shape, 0), lax.broadcasted_iota(jnp.int32, shape, 1)
    move = jnp.where(now == then % plan.group_rows * k + then // plan.group_rows, 1.0, 0.0).astype(BF)
    lines = nn(jnp.concatenate(lines, axis=0).astype(BF), move).astype(BF)
    if plan.shared:
        lines = lines[: plan.coded].astype(F32)
        parts = []
        for i in range(0, plan.width, LANES):
            parts += [pltpu.roll(lines[:, i : i + LANES], LANES // 2, 1), lines[:, i : i + LANES]]
        lines = jnp.concatenate(parts, axis=0)
    else:
        for target in firsts:
            target[first + len(pairs)] = lines
    shape = (plan.columns, plan.columns)
    same = lax.broadcasted_iota(jnp.int32, shape, 0) == lax.broadcasted_iota(jnp.int32, shape, 1)
    same = jnp.where(same, 1.0, 0.0).astype(BF)
    fill.wait()
    for j, pair in enumerate(pairs):
        for s in range(k):
            two = [raw_ref[level, s] for level in pair]
            two += [jnp.zeros((r, plan.columns), BF)] * (2 - len(two))
            turned_ref[s] = nt(same, jnp.concatenate(two, axis=0)).astype(BF)
        for target, (dp, dg) in zip(firsts, plan.chips):
            for s in range(k):
                for core in range(2):
                    column = ((part ^ dp) * plan.groups + (grid ^ dg) // 2 * 2 + core) * c
                    piece = turned_ref[s, pl.ds(pl.multiple_of(column, c), c), :]
                    if plan.shared and j == len(pairs) - 1:
                        low = lax.broadcasted_iota(jnp.int32, piece.shape, 1) < LANES // 2
                        here = lines[s * c : (s + 1) * c]
                        piece = jnp.where(low, piece.astype(F32), here).astype(BF)
                    target[first + j, s * c : (s + 1) * c, core * LANES : (core + 1) * LANES] = piece
    wait(copies)


def onehot(keys, first, rows):
    iota = lax.broadcasted_iota(jnp.int32, (rows, keys.shape[1]), 0)
    return jnp.where(iota == keys - first, 1.0, 0.0).astype(BF)


def cross(even, odd):
    half = even.shape[1] // 2
    low = lax.broadcasted_iota(jnp.int32, even.shape, 1) < half
    return (
        jnp.where(low, even, pltpu.roll(odd, half, 1)),
        jnp.where(low, pltpu.roll(even, half, 1), odd),
    )


def owners_at_once(plan):
    return min(plan.owners, max(2, ROWS_AT_ONCE // plan.rows))


def scatter(plan, sent, key_ref, level, levels_to, emit):
    c, per = plan.chunk, owners_at_once(plan)
    for pair in range(plan.groups // 2):
        given = []
        for g in (2 * pair, 2 * pair + 1):
            lanes = slice(g * plan.group_rows, (g + 1) * plan.group_rows)
            whole = jnp.concatenate([sent[s * c : (s + 1) * c, lanes] for s in range(plan.supers)], axis=1)
            super_to = key_ref[1, level, g : g + 1, :]
            given.append(
                jnp.concatenate(
                    [
                        whole * jnp.where(super_to == to * plan.supers + s, 1.0, 0.0).astype(BF)
                        for to in levels_to
                        for s in range(plan.supers)
                    ],
                    axis=0,
                )
            )
        for first in range(0, plan.owners, per):
            even, odd = [
                nt(
                    given[i],
                    onehot(
                        key_ref[0, level, 2 * pair + i : 2 * pair + i + 1, :],
                        first * plan.rows,
                        per * plan.rows,
                    ),
                )
                for i in range(2)
            ]
            for j in range(0, per, 2):
                at = slice(j * plan.rows, (j + 2) * plan.rows)
                one, two = cross(even[:, at], odd[:, at])
                for i, to in enumerate(levels_to):
                    rows = slice(i * plan.slab[0], (i + 1) * plan.slab[0])
                    emit(to, first + j, pair, one[rows])
                    emit(to, first + j + 1, pair, two[rows])


def gather(plan, froms, key_ref, level, done):
    c, per = plan.chunk, owners_at_once(plan)
    for pair in range(plan.groups // 2):
        lanes = slice(pair * LANES, (pair + 1) * LANES)
        total = [None, None]
        for first in range(0, plan.owners, per):
            given = [[], []]
            for _, slabs in froms:
                got = [[], []]
                for d in range(first, first + per, 2):
                    halves = cross(slabs[d][:, lanes].astype(F32), slabs[d + 1][:, lanes].astype(F32))
                    for i in range(2):
                        got[i].append(halves[i])
                for i in range(2):
                    given[i].append(jnp.concatenate(got[i], axis=1).astype(BF))
            for i in range(2):
                g = 2 * pair + i
                keys = key_ref[0, level, g : g + 1, :]
                super_to = key_ref[1, level, g : g + 1, :]
                found = nn(
                    jnp.concatenate(given[i], axis=0), onehot(keys, first * plan.rows, per * plan.rows)
                )
                at = 0
                for level_from, _ in froms:
                    for s in range(plan.supers):
                        term = jnp.where(super_to == level_from * plan.supers + s, found[at : at + c], 0.0)
                        total[i] = term if total[i] is None else total[i] + term
                        at += c
        for i in range(2):
            done(2 * pair + i, total[i])


def gate_kernel(*refs):
    pass


def stack_kernel(plan, counts, *refs):
    _, part, grid = plan.place()
    refs = list(refs)
    given = [[(refs.pop(0), first) for first in firsts] for firsts in counts]
    for parts, out in zip(given, refs[len(refs) - len(counts) :]):
        for i, (ref, first) in enumerate(parts):
            if len(out.shape) > 4 and len(ref.shape) > 3:
                out[(grid // 2) ^ i] = ref[...]
            elif len(out.shape) > 4:
                out[(grid // 2) ^ (i // plan.parts), part ^ (i % plan.parts)] = ref[...]
            else:
                out[part ^ i] = ref[first : first + out.shape[1]]


def forward_kernel(plan, level, part_of, added, unread, *refs):
    refs = list(refs)
    last, fresh = level == plan.levels - 1, level == 0
    c, halves = plan.chunk, plan.update_rows // plan.width
    key_ref = None if last or fresh else refs.pop(0)
    if not fresh:
        start_ref, *arrived = [refs.pop(0) for _ in range(1 + plan.owners)]
    more_ref = refs.pop(0) if added else None
    blocks = [refs.pop(0) for _ in range(2)]
    if fresh:
        del refs[:unread]
    out_ref = refs.pop(0)
    if last:
        solved_ref = refs.pop(0)
    else:
        sent_ref = refs.pop(0)
        slab_refs = [refs.pop(0) for _ in range(plan.owners)]
    if fresh:
        key_ref = refs.pop(0)
        next_refs = [refs.pop(0) for _ in range(plan.levels - 1)]
        pairs = (plan.levels + 1) // 2
        first = blocks[0].shape[2] - (not plan.shared) - pairs
        block = start_slab(plan, blocks, first, 0)
    else:
        block = start_ref[...] - arrived[0][...]
        for ref in arrived[1:]:
            block = block - ref[...].astype(F32)
    block = block.astype(BF)
    solved = jnp.concatenate(
        [nt(block[s * c : (s + 1) * c], joined(plan, blocks, part_of["fwd"], s)) for s in range(plan.supers)], axis=0
    )
    out_ref[...] = solved
    lowered = solved.astype(BF)
    if last:
        for s in range(plan.supers):
            at = slice(s * c, (s + 1) * c)
            solved_ref[at, :] = nt(lowered[at], joined(plan, blocks, part_of["inv"], s)).astype(BF)
        return
    if fresh:
        coded = [
            [coded_lines(plan, blocks, p, g, first + pairs) for p in range(plan.parts)]
            for g in range(plan.groups)
        ]
        for to in range(plan.levels - 1):
            for g in range(plan.groups):
                distance, row, super_to = [
                    jnp.concatenate([x[3 * to + i : 3 * to + i + 1] for x in coded[g]], axis=1) for i in range(3)
                ]
                key_ref[0, to, g : g + 1, :] = (distance * plan.rows + row).astype(jnp.int32)
                key_ref[1, to, g : g + 1, :] = super_to.astype(jnp.int32)
    for s in range(plan.supers):
        at = slice(s * c, (s + 1) * c)
        for half in range(halves):
            lanes = slice(half * plan.width, (half + 1) * plan.width)
            sent_ref[at, lanes] = nn(lowered[at], joined(plan, blocks, part_of["upd"] + half, s)).astype(BF)

    def emit(to, distance, pair, value):
        lanes = slice(pair * LANES, (pair + 1) * LANES)
        if more_ref is not None:
            value = value + more_ref[distance, :, lanes]
        slab_refs[distance][:, lanes] = value.astype(slab_refs[distance].dtype)

    scatter(plan, sent_ref[...], key_ref, level, [level + 1], emit)
    if fresh:
        for i, ref in enumerate(next_refs):
            ref[...] = start_slab(plan, blocks, first, i + 1)


def ahead_kernel(plan, level, *refs):
    sent, key_ref, more_ref = refs[:level], refs[level], refs[level + 1]
    for i, ref in enumerate(sent):

        def emit(to, distance, pair, value, first=i == 0):
            lanes = slice(pair * LANES, (pair + 1) * LANES)
            if not first:
                value = value + more_ref[distance, :, lanes]
            more_ref[distance, :, lanes] = value

        scatter(plan, ref[...], key_ref, i, [level + 1], emit)


def known_kernel(plan, level, froms, *refs):
    key_ref, out_ref = refs[0], refs[-1]
    slabs = [refs[1 + i * plan.owners : 1 + (i + 1) * plan.owners] for i in range(len(froms))]

    def done(g, value):
        out_ref[g] = value.astype(BF)

    gather(plan, list(zip(froms, slabs)), key_ref, level, done)


def backward_kernel(plan, level, part_of, known, *refs):
    refs = list(refs)
    key_ref = refs.pop(0)
    slabs = [refs.pop(0) for _ in range(plan.owners)]
    known_ref = refs.pop(0) if known else None
    forward_ref, *blocks, solved_ref = refs
    c, tall = plan.chunk, plan.group_rows // plan.rows
    pulled = [None] * plan.groups

    def done(g, value):
        if known:
            value = value + known_ref[g].astype(F32)
        pulled[g] = value.astype(BF)

    gather(plan, [(level + 1, slabs)], key_ref, level, done)
    for s in range(plan.supers):
        at = slice(s * c, (s + 1) * c)
        lanes = slice(s * plan.group_rows, (s + 1) * plan.group_rows)
        whole = jnp.concatenate([p[:, lanes] for p in pulled], axis=1)
        upper = nn(whole, joined(plan, blocks, part_of["upper"], s, tall))
        reduced = (forward_ref[at, :] - upper).astype(BF)
        solved_ref[at, :] = nt(reduced, joined(plan, blocks, part_of["inv"], s)).astype(BF)


def pieces_kernel(plan, *refs):
    _, part, grid = plan.place()
    slabs, outs = refs[: plan.levels], refs[plan.levels :]
    rows, half = plan.kept * plan.chunk, plan.rows
    low = lax.broadcasted_iota(jnp.int32, (rows, LANES), 1) < half
    for out, (dp, dg) in zip(outs, plan.blocks):
        first = pl.multiple_of((part ^ dp) * rows, rows)
        lane = pl.multiple_of((grid ^ dg) * half // LANES * LANES, LANES)
        turn = (grid ^ dg) * half % LANES
        for i in range(0, plan.levels, 2):
            two = [slab[pl.ds(first, rows), pl.ds(lane, LANES)].astype(F32) for slab in slabs[i : i + 2]]
            one = pltpu.roll(two[0], turn, 1)
            if len(two) > 1:
                one = jnp.where(low, one, pltpu.roll(two[1], half - turn, 1))
            out[i // 2] = one.astype(BF)


def result_kernel(plan, *refs):
    _, part, grid = plan.place()
    refs = list(refs)
    scratch, out = refs.pop(), refs.pop()
    c = plan.chunk
    shape = (plan.rows, LANES)
    lane = lax.broadcasted_iota(jnp.int32, shape, 1)
    row = lax.broadcasted_iota(jnp.int32, shape, 0)
    picks = [jnp.where(lane == row + i * plan.rows, 1.0, 0.0).astype(BF) for i in range(2)]
    for k in range(plan.kept):
        for ref, (dp, dg) in zip(refs, plan.blocks):
            at = ((part ^ dp) * plan.groups + (grid ^ dg)) * c
            for i in range((plan.levels + 1) // 2):
                scratch[i, k, pl.ds(pl.multiple_of(at, c), c), :] = ref[i, k * c : (k + 1) * c, :]
    for level in range(plan.levels):
        for k in range(plan.kept):
            out[level, k] = nt(picks[level % 2], scratch[level // 2, k]).astype(BF)


VM = pl.BlockSpec(memory_space=pltpu.VMEM)
ANY = pl.BlockSpec(memory_space=pltpu.HBM)
UNREAD = pl.BlockSpec(memory_space=pl.ANY)


def call(body, args, specs, outs, scratch, flops, moved, vmem=VMEM_BYTES):
    return pl.pallas_call(
        body,
        in_specs=specs,
        out_specs=[VM] * len(outs),
        out_shape=[jax.ShapeDtypeStruct(shape, dtype) for shape, dtype in outs],
        scratch_shapes=scratch,
        compiler_params=pltpu.CompilerParams(vmem_limit_bytes=vmem),
        cost_estimate=pl.CostEstimate(flops=flops, bytes_accessed=moved, transcendentals=0),
    )(*args)


def gate(x, *others):
    return pl.pallas_call(
        gate_kernel,
        in_specs=[UNREAD] * (1 + len(others)),
        out_specs=UNREAD,
        out_shape=jax.ShapeDtypeStruct(x.shape, x.dtype),
        input_output_aliases={0: 0},
        compiler_params=pltpu.CompilerParams(vmem_limit_bytes=2**20),
        cost_estimate=pl.CostEstimate(flops=0, bytes_accessed=0, transcendentals=0),
    )(x, *others)


def stack(plan, jobs, *others):
    args = [x for parts, _ in jobs for x, _ in parts]
    return call(
        functools.partial(stack_kernel, plan, [[first for _, first in parts] for parts, _ in jobs]),
        args + list(others), [VM] * len(args) + [UNREAD] * len(others),
        [(shape, BF) for _, shape in jobs], [], 1, 2**19,
    )


def solve(plan, rhs, fwd_inv, bwd_inv, upd_t, bwd_t, dest_owner, dest_row):
    levels, owners = plan.levels, plan.owners
    owner_at, part, grid = plan.place()

    def over_leaf(x, step):
        return lax.ppermute(x, "leaf", [(i, i ^ step) for i in range(plan.leaves)])

    def over_grid(x, step):
        return lax.ppermute(x, "grid", [(i, i ^ step) for i in range(plan.groups)])

    def from_owners(x):
        got = {d: over_leaf(x[d], d * plan.parts) for d in reversed(range(1, owners))}
        return [x[0]] + [got[d] for d in range(1, owners)]

    def swap(x, dp, dg):
        if (dp, dg) == (0, 0):
            return x
        g = plan.groups
        moves = [(i, ((i // g) ^ dp) * g + ((i % g) ^ dg)) for i in range(plan.leaves * g)]
        return lax.ppermute(x, ("leaf", "grid"), moves)

    top, every = levels - 1, slice(None)
    halves = plan.update_rows // plan.width
    tall = plan.group_rows // plan.rows

    def parts_of(name, level):
        if name == "upd":
            return [(2, (level, every, every, pl.ds(h * plan.width, plan.width))) for h in range(halves)]
        if name == "upper":
            return [(3, (level, every, pl.ds(h * plan.rows, plan.rows))) for h in range(tall)]
        return [(dict(fwd=0, inv=1)[name], (level,))]

    names = [[("fwd", level), ("upd", level)] for level in range(top)]
    names.append([("fwd", top), ("inv", top)])
    names += [[("upper", level), ("inv", level)] for level in reversed(range(top))]
    where, layouts = {}, []
    for number, chunk in enumerate(names):
        layouts.append([])
        for name, level in chunk:
            where[name, level] = (number, len(layouts[-1]))
            layouts[-1] += parts_of(name, level)
    pairs = [tuple(range(i, min(i + 2, levels))) for i in range(0, levels, 2)]
    slab = (plan.rows, plan.width)
    matrices_given = (fwd_inv, bwd_inv, upd_t, bwd_t)

    ways, extra = len(plan.chips), len(pairs) + (not plan.shared)
    *given, second = call(
        functools.partial(first_kernel, plan, layouts[0], layouts[1], pairs),
        [*matrices_given, rhs, dest_owner.reshape(dest_row.shape), dest_row],
        [ANY] * 5 + [VM] * 2,
        [((len(layouts[0]) * plan.kept + extra,) + slab, BF)] * ways
        + [((len(layouts[1]) * plan.kept,) + slab, BF)],
        [
            pltpu.VMEM(rhs.shape, BF),
            pltpu.VMEM((plan.kept, plan.columns, LANES), BF),
            pltpu.SemaphoreType.DMA((1 + ways * len(layouts[0]) + len(layouts[1]),)),
        ],
        1, 2**20, PACK_VMEM_BYTES,
    )
    sizes = [len(x) * plan.kept for x in layouts]
    later = levels + 1
    grouped = [layouts[2], sum(layouts[3:later], []), sum(layouts[later:], [])]
    owned = call(
        functools.partial(pack_kernel, plan, grouped),
        [*matrices_given, given[0]], [ANY] * 4 + [UNREAD],
        [((len(x) * plan.kept,) + slab, BF) for x in grouped],
        [pltpu.SemaphoreType.DMA((sum(len(x) for x in grouped),))],
        1, 2**20,
    )
    got = {chip: swap(x, *chip) for chip, x in zip(plan.chips, given)}
    def to_part(x):
        return [x] + [over_leaf(x, dp) for dp in range(1, plan.parts)]

    def to_chip(x):
        return [x] + [over_grid(x, dg) for dg in range(2, plan.groups, 2)]

    second = to_part(second)
    second = second + sum([[over_grid(x, dg) for x in second] for dg in range(2, plan.groups, 2)], [])
    third = to_part(owned[0])
    shape = (plan.groups // 2, plan.parts)
    begun = stack(
        plan,
        [
            ([(got[chip], 0) for chip in plan.chips], shape + given[0].shape),
            ([(x, 0) for x in second], shape + second[0].shape),
            ([(x, 0) for x in third], (plan.parts,) + third[0].shape),
        ],
    )
    chunks = {number: [begun[number], over_grid(begun[number], 1)] for number in range(2)}
    from_part, two = {}, {2: [(x, 0) for x in to_chip(begun[2])]}

    def slices(first, last, x):
        parts, at = to_part(x), 0
        for number in range(first, last):
            from_part[number] = [(part, at) for part in parts]
            at += sizes[number]
        return parts[-1]

    marks = [slices(3, later, gate(owned[1], begun[2]))]
    before_first = []

    def advance(stage, mark):
        if stage == 1:
            slices(later, len(layouts), gate(owned[2], mark, marks[-1]))
        jobs, done = [], []
        if stage + 1 in two:
            shape = (plan.groups // 2, plan.parts, sizes[stage + 1]) + slab
            jobs.append((two[stage + 1], shape))
            done.append(stage + 1)
        if stage + 2 in from_part:
            jobs.append((from_part[stage + 2], (plan.parts, sizes[stage + 2]) + slab))
            done.append(stage + 2)
        for x, number in zip(stack(plan, jobs, mark) if jobs else [], done):
            if number == stage + 1:
                chunks[number] = [x, over_grid(x, 1)]
            else:
                two[number] = [(x, 0) for x in to_chip(x)]

    def matrices(level, wanted):
        (number,) = {where[name, level][0] for name in wanted}
        return chunks[number], {name: where[name, level][1] for name in wanted}

    full = (plan.parts, plan.kept, plan.groups, plan.rows, plan.width)
    slab_bytes = plan.slab[0] * plan.slab[1] * 2
    one_pass = 2 * plan.slab[0] * plan.slab[1] * plan.sources * plan.groups * max(1, owners // 4)

    forward_out, sent, starts, arrived, more = [], [], {}, [], None
    for level in range(levels):
        last, fresh = level == top, level == 0
        blocks, part_of = matrices(level, ["fwd", "inv" if last else "upd"])
        count = len(blocks)
        args, specs = [], []
        if not last and not fresh:
            args.append(keys)
            specs.append(VM)
        if not fresh:
            args += [starts[level]] + arrived
            specs += [VM] * (1 + owners)
        if more is not None and not last:
            args.append(more)
            specs.append(VM)
        args += blocks
        specs += [VM] * count
        if fresh:
            args += before_first
            specs += [UNREAD] * len(before_first)
        outs = [(plan.slab, F32)]
        if last:
            outs.append((plan.slab, BF))
        else:
            outs.append(((plan.slab[0], plan.update_rows), BF))
            outs += [(plan.slab, F32)] + [(plan.slab, BF)] * (owners - 1)
        if fresh:
            outs.append(((2, levels - 1, plan.groups, plan.sources), jnp.int32))
            outs += [(plan.slab, F32)] * top
        got = call(
            functools.partial(
                forward_kernel, plan, level, part_of, more is not None and not last,
                len(before_first),
            ),
            args, specs, outs, [], one_pass, 24 * slab_bytes,
        )
        forward_out.append(got[0])
        if last:
            solved = got[1]
            break
        sent.append(got[1])
        if fresh:
            keys = got[-1 - top]
            starts.update(zip(range(1, levels), got[-top:]))
        arrived = from_owners(got[2 : 2 + owners])
        advance(level, got[1])
        more = None
        if level + 1 < top:
            (more,) = call(
                functools.partial(ahead_kernel, plan, level + 1),
                sent + [keys], [VM] * (len(sent) + 1), [((owners,) + plan.slab, F32)], [],
                one_pass * len(sent), 16 * slab_bytes,
            )

    solutions = {top: solved}
    everywhere = {}
    for level in reversed(range(top)):
        above = solutions[level + 1]
        everywhere[level + 1] = from_owners([above] * owners)
        froms = list(range(level + 2, levels))
        known = []
        if froms:
            slabs = sum([everywhere[f] for f in froms], [])
            known = call(
                functools.partial(known_kernel, plan, level, froms),
                [keys] + slabs, [VM] * (1 + len(slabs)),
                [((plan.groups, plan.chunk, plan.sources), BF)], [],
                one_pass * len(froms), 16 * slab_bytes,
            )
        advance(levels + top - level - 2, above)
        blocks, part_of = matrices(level, ["upper", "inv"])
        args = [keys] + everywhere[level + 1] + list(known) + [forward_out[level]]
        (solutions[level],) = call(
            functools.partial(backward_kernel, plan, level, part_of, bool(froms)),
            args + blocks, [VM] * (len(args) + len(blocks)), [(plan.slab, BF)], [],
            one_pass, 24 * slab_bytes,
        )

    piece = ((levels + 1) // 2, plan.kept * plan.chunk, LANES)
    own = call(
        functools.partial(pieces_kernel, plan),
        [solutions[level] for level in range(levels)], [VM] * levels,
        [(piece, BF)] * len(plan.blocks), [], 1, 8 * slab_bytes,
    )
    far_first = sorted(range(len(plan.blocks)), key=lambda i: -sum(b.bit_count() for b in plan.blocks[i]))
    theirs = {i: swap(own[i], *plan.blocks[i]) for i in far_first}
    theirs = [theirs[i] for i in range(len(own))]
    (result,) = call(
        functools.partial(result_kernel, plan),
        theirs, [VM] * len(theirs), [(rhs.shape, BF)],
        [pltpu.VMEM(((levels + 1) // 2, plan.kept, plan.columns, LANES), BF)], 1, 8 * slab_bytes,
    )
    return result


def solution(mesh):
    def local(rhs, fwd_inv, bwd_inv, upd_t, bwd_t, dest_owner, dest_row):
        plan = Plan(mesh, rhs, upd_t, bwd_t)
        return solve(plan, rhs, fwd_inv, bwd_inv, upd_t, bwd_t, dest_owner, dest_row)

    rows = P(None, "leaf", "grid", None)
    placed = (rows, rows, rows, rows, rows, P(None, "leaf", "grid", None, None), rows)
    return jax.shard_map(local, mesh=mesh, in_specs=placed, out_specs=rows, check_vma=False)
```

```python
import functools

import jax
import jax.numpy as jnp
from jax import lax
from jax.experimental import pallas as pl
from jax.experimental.pallas import tpu as pltpu
from jax.sharding import PartitionSpec as P

BF = jnp.bfloat16
F32 = jnp.float32
LANES = 128
ROWS_AT_ONCE = 256
VMEM_BYTES = 16 * 1024 * 1024
PACK_VMEM_BYTES = 60 * 1024 * 1024


def nn(a, b):
    return lax.dot_general(a, b, (((1,), (0,)), ((), ())), preferred_element_type=F32)


def nt(a, b):
    return lax.dot_general(a, b, (((1,), (1,)), ((), ())), preferred_element_type=F32)


class Plan:
    def __init__(self, mesh, rhs, upd_t, bwd_t):
        self.levels, self.kept, self.rows, self.columns = rhs.shape
        self.leaves, self.groups = mesh.shape["leaf"], mesh.shape["grid"]
        self.parts = 2 if self.leaves % 2 == 0 else 1
        self.owners = self.leaves // self.parts
        self.supers = self.parts * self.kept
        self.chunk = self.columns // (self.groups * self.parts)
        self.width = self.rows * self.groups
        self.update_rows = upd_t.shape[3]
        self.group_rows = bwd_t.shape[2]
        self.slab = (self.supers * self.chunk, self.width)
        self.chips = [(dp, dg) for dg in range(0, self.groups, 2) for dp in range(self.parts)]
        self.shared = self.levels % 2 == 1
        self.coded = -(-3 * (self.levels - 1) // 16) * 16
        self.sources = self.supers * self.group_rows
        self.blocks = [(dp, dg) for dp in range(self.parts) for dg in range(self.groups)]

    def place(self):
        leaf, grid = lax.axis_index("leaf"), lax.axis_index("grid")
        return leaf // self.parts, leaf % self.parts, grid


def wait(group):
    for copy in group:
        copy.wait()


def block_of(plan, stacks, p, g, row):
    same = lax.axis_index("grid") % 2 == g % 2
    return jnp.where(same, stacks[0][g // 2, p, row], stacks[1][g // 2, p, row])


def joined(plan, stacks, slab, s, count=1):
    p, k = s // plan.kept, s % plan.kept
    rows = [
        block_of(plan, stacks, p, g, (slab + i) * plan.kept + k)
        for g in range(plan.groups)
        for i in range(count)
    ]
    return jnp.concatenate(rows, axis=0)


def start_slab(plan, stacks, first, level):
    low_core = lax.axis_index("grid") % 2 == 0

    def piece(p, g):
        both = block_of(plan, stacks, p, g, first + level // 2).astype(F32)
        return jnp.where(low_core, both[:, :LANES], both[:, LANES:])

    out = []
    for pair in range(plan.groups // 2):
        halves = [cross(piece(p, 2 * pair), piece(p, 2 * pair + 1))[level % 2] for p in range(plan.parts)]
        out.append(jnp.concatenate(halves, axis=0))
    return jnp.concatenate(out, axis=1)


def coded_lines(plan, stacks, p, g, end):
    if not plan.shared:
        return block_of(plan, stacks, p, g, end)[: plan.coded].astype(F32)
    both = block_of(plan, stacks, p, g, end - 1).astype(F32)
    lines = jnp.where(lax.axis_index("grid") % 2 == 0, both[:, :LANES], both[:, LANES:])
    low = lax.broadcasted_iota(jnp.int32, (plan.coded, LANES), 1) < LANES // 2
    out = []
    for i in range(0, 2 * plan.width // LANES, 2):
        one, two = [lines[(i + j) * plan.coded : (i + j + 1) * plan.coded] for j in range(2)]
        out.append(jnp.where(low, pltpu.roll(one, LANES // 2, 1), two))
    return jnp.concatenate(out, axis=1)


def copy_matrices(plan, sources, layout, target, sems, at):
    copies = []
    for i, (source, index) in enumerate(layout):
        to = target.at[pl.ds(i * plan.kept, plan.kept)]
        copies.append(pltpu.make_async_copy(sources[source].at[index], to, sems.at[at + i]))
        copies[-1].start()
    return copies


def pack_kernel(plan, layouts, *refs):
    sources, targets, sems = refs[:4], refs[-1 - len(layouts) : -1], refs[-1]
    copies = []
    for layout, target in zip(layouts, targets):
        copies += copy_matrices(plan, sources, layout, target, sems, len(copies))
    wait(copies)


def first_kernel(plan, layout, second, pairs, *refs):
    refs = list(refs)
    sources = [refs.pop(0) for _ in range(4)]
    rhs_ref, owner_ref, row_ref = [refs.pop(0) for _ in range(3)]
    firsts, second_ref = [refs.pop(0) for _ in plan.chips], refs.pop(0)
    raw_ref, turned_ref, sems = refs
    owner_at, part, grid = plan.place()
    k, r, c = plan.kept, plan.rows, plan.chunk
    fill = pltpu.make_async_copy(rhs_ref, raw_ref, sems.at[0])
    fill.start()
    copies = []
    for target in firsts:
        copies += copy_matrices(plan, sources, layout, target, sems, 1 + len(copies))
    copies += copy_matrices(plan, sources, second, second_ref, sems, 1 + len(copies))
    first = len(layout) * k
    leaf_to, row_to = [
        jnp.concatenate([ref[level, 0] for level in range(plan.levels - 1)], axis=0) for ref in (owner_ref, row_ref)
    ]
    block_to = row_to // r
    super_to = (block_to // k * plan.parts + leaf_to % plan.parts) * k + block_to % k
    fields = [(leaf_to // plan.parts) ^ owner_at, row_to % r, super_to]
    lines = [x[i : i + 1].astype(F32) for i in range(plan.levels - 1) for x in fields]
    lines.append(jnp.zeros((r - len(lines), plan.width), F32))
    shape = (plan.width, plan.width)
    now, then = lax.broadcasted_iota(jnp.int32, shape, 0), lax.broadcasted_iota(jnp.int32, shape, 1)
    move = jnp.where(now == then % plan.group_rows * k + then // plan.group_rows, 1.0, 0.0).astype(BF)
    lines = nn(jnp.concatenate(lines, axis=0).astype(BF), move).astype(BF)
    if plan.shared:
        lines = lines[: plan.coded].astype(F32)
        parts = []
        for i in range(0, plan.width, LANES):
            parts += [pltpu.roll(lines[:, i : i + LANES], LANES // 2, 1), lines[:, i : i + LANES]]
        lines = jnp.concatenate(parts, axis=0)
    else:
        for target in firsts:
            target[first + len(pairs)] = lines
    shape = (plan.columns, plan.columns)
    same = lax.broadcasted_iota(jnp.int32, shape, 0) == lax.broadcasted_iota(jnp.int32, shape, 1)
    same = jnp.where(same, 1.0, 0.0).astype(BF)
    fill.wait()
    for j, pair in enumerate(pairs):
        for s in range(k):
            two = [raw_ref[level, s] for level in pair]
            two += [jnp.zeros((r, plan.columns), BF)] * (2 - len(two))
            turned_ref[s] = nt(same, jnp.concatenate(two, axis=0)).astype(BF)
        for target, (dp, dg) in zip(firsts, plan.chips):
            for s in range(k):
                for core in range(2):
                    column = ((part ^ dp) * plan.groups + (grid ^ dg) // 2 * 2 + core) * c
                    piece = turned_ref[s, pl.ds(pl.multiple_of(column, c), c), :]
                    if plan.shared and j == len(pairs) - 1:
                        low = lax.broadcasted_iota(jnp.int32, piece.shape, 1) < LANES // 2
                        here = lines[s * c : (s + 1) * c]
                        piece = jnp.where(low, piece.astype(F32), here).astype(BF)
                    target[first + j, s * c : (s + 1) * c, core * LANES : (core + 1) * LANES] = piece
    wait(copies)


def onehot(keys, first, rows):
    iota = lax.broadcasted_iota(jnp.int32, (rows, keys.shape[1]), 0)
    return jnp.where(iota == keys - first, 1.0, 0.0).astype(BF)


def cross(even, odd):
    half = even.shape[1] // 2
    low = lax.broadcasted_iota(jnp.int32, even.shape, 1) < half
    return (
        jnp.where(low, even, pltpu.roll(odd, half, 1)),
        jnp.where(low, pltpu.roll(even, half, 1), odd),
    )


def owners_at_once(plan):
    return min(plan.owners, max(2, ROWS_AT_ONCE // plan.rows))


def scatter(plan, sent, key_ref, level, levels_to, emit):
    c, per = plan.chunk, owners_at_once(plan)
    for pair in range(plan.groups // 2):
        given = []
        for g in (2 * pair, 2 * pair + 1):
            lanes = slice(g * plan.group_rows, (g + 1) * plan.group_rows)
            whole = jnp.concatenate([sent[s * c : (s + 1) * c, lanes] for s in range(plan.supers)], axis=1)
            super_to = key_ref[1, level, g : g + 1, :]
            given.append(
                jnp.concatenate(
                    [
                        whole * jnp.where(super_to == to * plan.supers + s, 1.0, 0.0).astype(BF)
                        for to in levels_to
                        for s in range(plan.supers)
                    ],
                    axis=0,
                )
            )
        for first in range(0, plan.owners, per):
            even, odd = [
                nt(
                    given[i],
                    onehot(
                        key_ref[0, level, 2 * pair + i : 2 * pair + i + 1, :],
                        first * plan.rows,
                        per * plan.rows,
                    ),
                )
                for i in range(2)
            ]
            for j in range(0, per, 2):
                at = slice(j * plan.rows, (j + 2) * plan.rows)
                one, two = cross(even[:, at], odd[:, at])
                for i, to in enumerate(levels_to):
                    rows = slice(i * plan.slab[0], (i + 1) * plan.slab[0])
                    emit(to, first + j, pair, one[rows])
                    emit(to, first + j + 1, pair, two[rows])


def gather(plan, froms, key_ref, level, done):
    c, per = plan.chunk, owners_at_once(plan)
    for pair in range(plan.groups // 2):
        lanes = slice(pair * LANES, (pair + 1) * LANES)
        total = [None, None]
        for first in range(0, plan.owners, per):
            given = [[], []]
            for _, slabs in froms:
                got = [[], []]
                for d in range(first, first + per, 2):
                    halves = cross(slabs[d][:, lanes].astype(F32), slabs[d + 1][:, lanes].astype(F32))
                    for i in range(2):
                        got[i].append(halves[i])
                for i in range(2):
                    given[i].append(jnp.concatenate(got[i], axis=1).astype(BF))
            for i in range(2):
                g = 2 * pair + i
                keys = key_ref[0, level, g : g + 1, :]
                super_to = key_ref[1, level, g : g + 1, :]
                found = nn(
                    jnp.concatenate(given[i], axis=0), onehot(keys, first * plan.rows, per * plan.rows)
                )
                at = 0
                for level_from, _ in froms:
                    for s in range(plan.supers):
                        term = jnp.where(super_to == level_from * plan.supers + s, found[at : at + c], 0.0)
                        total[i] = term if total[i] is None else total[i] + term
                        at += c
        for i in range(2):
            done(2 * pair + i, total[i])


def gate_kernel(*refs):
    pass


def stack_kernel(plan, counts, *refs):
    _, part, grid = plan.place()
    refs = list(refs)
    given = [[(refs.pop(0), first) for first in firsts] for firsts in counts]
    for parts, out in zip(given, refs[len(refs) - len(counts) :]):
        for i, (ref, first) in enumerate(parts):
            if len(out.shape) > 4 and len(ref.shape) > 3:
                out[(grid // 2) ^ i] = ref[...]
            elif len(out.shape) > 4:
                out[(grid // 2) ^ (i // plan.parts), part ^ (i % plan.parts)] = ref[...]
            else:
                out[part ^ i] = ref[first : first + out.shape[1]]


def forward_kernel(plan, level, part_of, added, unread, *refs):
    refs = list(refs)
    last, fresh = level == plan.levels - 1, level == 0
    c, halves = plan.chunk, plan.update_rows // plan.width
    key_ref = None if last or fresh else refs.pop(0)
    if not fresh:
        start_ref, *arrived = [refs.pop(0) for _ in range(1 + plan.owners)]
    more_ref = refs.pop(0) if added else None
    blocks = [refs.pop(0) for _ in range(2)]
    if fresh:
        del refs[:unread]
    out_ref = refs.pop(0)
    if last:
        solved_ref = refs.pop(0)
    else:
        sent_ref = refs.pop(0)
        slab_refs = [refs.pop(0) for _ in range(plan.owners)]
    if fresh:
        key_ref = refs.pop(0)
        next_refs = [refs.pop(0) for _ in range(plan.levels - 1)]
        pairs = (plan.levels + 1) // 2
        first = blocks[0].shape[2] - (not plan.shared) - pairs
        block = start_slab(plan, blocks, first, 0)
    else:
        block = start_ref[...] - arrived[0][...]
        for ref in arrived[1:]:
            block = block - ref[...].astype(F32)
    block = block.astype(BF)
    solved = jnp.concatenate(
        [nt(block[s * c : (s + 1) * c], joined(plan, blocks, part_of["fwd"], s)) for s in range(plan.supers)], axis=0
    )
    out_ref[...] = solved
    lowered = solved.astype(BF)
    if last:
        for s in range(plan.supers):
            at = slice(s * c, (s + 1) * c)
            solved_ref[at, :] = nt(lowered[at], joined(plan, blocks, part_of["inv"], s)).astype(BF)
        return
    if fresh:
        coded = [
            [coded_lines(plan, blocks, p, g, first + pairs) for p in range(plan.parts)]
            for g in range(plan.groups)
        ]
        for to in range(plan.levels - 1):
            for g in range(plan.groups):
                distance, row, super_to = [
                    jnp.concatenate([x[3 * to + i : 3 * to + i + 1] for x in coded[g]], axis=1) for i in range(3)
                ]
                key_ref[0, to, g : g + 1, :] = (distance * plan.rows + row).astype(jnp.int32)
                key_ref[1, to, g : g + 1, :] = super_to.astype(jnp.int32)
    for s in range(plan.supers):
        at = slice(s * c, (s + 1) * c)
        for half in range(halves):
            lanes = slice(half * plan.width, (half + 1) * plan.width)
            sent_ref[at, lanes] = nn(lowered[at], joined(plan, blocks, part_of["upd"] + half, s)).astype(BF)

    def emit(to, distance, pair, value):
        lanes = slice(pair * LANES, (pair + 1) * LANES)
        if more_ref is not None:
            value = value + more_ref[distance, :, lanes]
        slab_refs[distance][:, lanes] = value.astype(slab_refs[distance].dtype)

    scatter(plan, sent_ref[...], key_ref, level, [level + 1], emit)
    if fresh:
        for i, ref in enumerate(next_refs):
            ref[...] = start_slab(plan, blocks, first, i + 1)


def ahead_kernel(plan, level, *refs):
    sent, key_ref, more_ref = refs[:level], refs[level], refs[level + 1]
    for i, ref in enumerate(sent):

        def emit(to, distance, pair, value, first=i == 0):
            lanes = slice(pair * LANES, (pair + 1) * LANES)
            if not first:
                value = value + more_ref[distance, :, lanes]
            more_ref[distance, :, lanes] = value

        scatter(plan, ref[...], key_ref, i, [level + 1], emit)


def known_kernel(plan, level, froms, *refs):
    key_ref, out_ref = refs[0], refs[-1]
    slabs = [refs[1 + i * plan.owners : 1 + (i + 1) * plan.owners] for i in range(len(froms))]

    def done(g, value):
        out_ref[g] = value.astype(BF)

    gather(plan, list(zip(froms, slabs)), key_ref, level, done)


def backward_kernel(plan, level, part_of, known, *refs):
    refs = list(refs)
    key_ref = refs.pop(0)
    slabs = [refs.pop(0) for _ in range(plan.owners)]
    known_ref = refs.pop(0) if known else None
    forward_ref, *blocks, solved_ref = refs
    c, tall = plan.chunk, plan.group_rows // plan.rows
    pulled = [None] * plan.groups

    def done(g, value):
        if known:
            value = value + known_ref[g].astype(F32)
        pulled[g] = value.astype(BF)

    gather(plan, [(level + 1, slabs)], key_ref, level, done)
    for s in range(plan.supers):
        at = slice(s * c, (s + 1) * c)
        lanes = slice(s * plan.group_rows, (s + 1) * plan.group_rows)
        whole = jnp.concatenate([p[:, lanes] for p in pulled], axis=1)
        upper = nn(whole, joined(plan, blocks, part_of["upper"], s, tall))
        reduced = (forward_ref[at, :] - upper).astype(BF)
        solved_ref[at, :] = nt(reduced, joined(plan, blocks, part_of["inv"], s)).astype(BF)


def pieces_kernel(plan, *refs):
    _, part, grid = plan.place()
    slabs, outs = refs[: plan.levels], refs[plan.levels :]
    rows, half = plan.kept * plan.chunk, plan.rows
    low = lax.broadcasted_iota(jnp.int32, (rows, LANES), 1) < half
    for out, (dp, dg) in zip(outs, plan.blocks):
        first = pl.multiple_of((part ^ dp) * rows, rows)
        lane = pl.multiple_of((grid ^ dg) * half // LANES * LANES, LANES)
        turn = (grid ^ dg) * half % LANES
        for i in range(0, plan.levels, 2):
            two = [slab[pl.ds(first, rows), pl.ds(lane, LANES)].astype(F32) for slab in slabs[i : i + 2]]
            one = pltpu.roll(two[0], turn, 1)
            if len(two) > 1:
                one = jnp.where(low, one, pltpu.roll(two[1], half - turn, 1))
            out[i // 2] = one.astype(BF)


def result_kernel(plan, *refs):
    _, part, grid = plan.place()
    refs = list(refs)
    scratch, out = refs.pop(), refs.pop()
    c = plan.chunk
    shape = (plan.rows, LANES)
    lane = lax.broadcasted_iota(jnp.int32, shape, 1)
    row = lax.broadcasted_iota(jnp.int32, shape, 0)
    picks = [jnp.where(lane == row + i * plan.rows, 1.0, 0.0).astype(BF) for i in range(2)]
    for k in range(plan.kept):
        for ref, (dp, dg) in zip(refs, plan.blocks):
            at = ((part ^ dp) * plan.groups + (grid ^ dg)) * c
            for i in range((plan.levels + 1) // 2):
                scratch[i, k, pl.ds(pl.multiple_of(at, c), c), :] = ref[i, k * c : (k + 1) * c, :]
    for level in range(plan.levels):
        for k in range(plan.kept):
            out[level, k] = nt(picks[level % 2], scratch[level // 2, k]).astype(BF)


VM = pl.BlockSpec(memory_space=pltpu.VMEM)
ANY = pl.BlockSpec(memory_space=pltpu.HBM)
UNREAD = pl.BlockSpec(memory_space=pl.ANY)


def call(body, args, specs, outs, scratch, flops, moved, vmem=VMEM_BYTES):
    return pl.pallas_call(
        body,
        in_specs=specs,
        out_specs=[VM] * len(outs),
        out_shape=[jax.ShapeDtypeStruct(shape, dtype) for shape, dtype in outs],
        scratch_shapes=scratch,
        compiler_params=pltpu.CompilerParams(vmem_limit_bytes=vmem),
        cost_estimate=pl.CostEstimate(flops=flops, bytes_accessed=moved, transcendentals=0),
    )(*args)


def gate(x, *others, flops=0):
    return pl.pallas_call(
        gate_kernel,
        in_specs=[UNREAD] * (1 + len(others)),
        out_specs=UNREAD,
        out_shape=jax.ShapeDtypeStruct(x.shape, x.dtype),
        input_output_aliases={0: 0},
        compiler_params=pltpu.CompilerParams(vmem_limit_bytes=2**20),
        cost_estimate=pl.CostEstimate(flops=flops, bytes_accessed=0, transcendentals=0),
    )(x, *others)


def stack(plan, jobs, *others):
    args = [x for parts, _ in jobs for x, _ in parts]
    return call(
        functools.partial(stack_kernel, plan, [[first for _, first in parts] for parts, _ in jobs]),
        args + list(others), [VM] * len(args) + [UNREAD] * len(others),
        [(shape, BF) for _, shape in jobs], [], 1, 2**19,
    )


def solve(plan, rhs, fwd_inv, bwd_inv, upd_t, bwd_t, dest_owner, dest_row):
    levels, owners = plan.levels, plan.owners
    owner_at, part, grid = plan.place()

    def over_leaf(x, step):
        return lax.ppermute(x, "leaf", [(i, i ^ step) for i in range(plan.leaves)])

    def over_grid(x, step):
        return lax.ppermute(x, "grid", [(i, i ^ step) for i in range(plan.groups)])

    def from_owners(x):
        got = {d: over_leaf(x[d], d * plan.parts) for d in reversed(range(1, owners))}
        return [x[0]] + [got[d] for d in range(1, owners)]

    def swap(x, dp, dg):
        if (dp, dg) == (0, 0):
            return x
        g = plan.groups
        moves = [(i, ((i // g) ^ dp) * g + ((i % g) ^ dg)) for i in range(plan.leaves * g)]
        return lax.ppermute(x, ("leaf", "grid"), moves)

    top, every = levels - 1, slice(None)
    halves = plan.update_rows // plan.width
    tall = plan.group_rows // plan.rows

    def parts_of(name, level):
        if name == "upd":
            return [(2, (level, every, every, pl.ds(h * plan.width, plan.width))) for h in range(halves)]
        if name == "upper":
            return [(3, (level, every, pl.ds(h * plan.rows, plan.rows))) for h in range(tall)]
        return [(dict(fwd=0, inv=1)[name], (level,))]

    names = [[("fwd", level), ("upd", level)] for level in range(top)]
    names.append([("fwd", top), ("inv", top)])
    names += [[("upper", level), ("inv", level)] for level in reversed(range(top))]
    where, layouts = {}, []
    for number, chunk in enumerate(names):
        layouts.append([])
        for name, level in chunk:
            where[name, level] = (number, len(layouts[-1]))
            layouts[-1] += parts_of(name, level)
    pairs = [tuple(range(i, min(i + 2, levels))) for i in range(0, levels, 2)]
    slab = (plan.rows, plan.width)
    matrices_given = (fwd_inv, bwd_inv, upd_t, bwd_t)

    ways, extra = len(plan.chips), len(pairs) + (not plan.shared)
    *given, second = call(
        functools.partial(first_kernel, plan, layouts[0], layouts[1], pairs),
        [*matrices_given, rhs, dest_owner.reshape(dest_row.shape), dest_row],
        [ANY] * 5 + [VM] * 2,
        [((len(layouts[0]) * plan.kept + extra,) + slab, BF)] * ways
        + [((len(layouts[1]) * plan.kept,) + slab, BF)],
        [
            pltpu.VMEM(rhs.shape, BF),
            pltpu.VMEM((plan.kept, plan.columns, LANES), BF),
            pltpu.SemaphoreType.DMA((1 + ways * len(layouts[0]) + len(layouts[1]),)),
        ],
        1, 2**20, PACK_VMEM_BYTES,
    )
    sizes = [len(x) * plan.kept for x in layouts]
    later = levels + 1
    grouped = [layouts[2], sum(layouts[3:later], []), sum(layouts[later:], [])]
    owned = call(
        functools.partial(pack_kernel, plan, grouped),
        [*matrices_given, given[0]], [ANY] * 4 + [UNREAD],
        [((len(x) * plan.kept,) + slab, BF) for x in grouped],
        [pltpu.SemaphoreType.DMA((sum(len(x) for x in grouped),))],
        1, 2**20,
    )
    got = {chip: swap(x, *chip) for chip, x in zip(plan.chips, given)}
    def to_part(x):
        return [x] + [over_leaf(x, dp) for dp in range(1, plan.parts)]

    def to_chip(x):
        return [x] + [over_grid(x, dg) for dg in range(2, plan.groups, 2)]

    second = to_part(second)
    second = second + sum([[over_grid(x, dg) for x in second] for dg in range(2, plan.groups, 2)], [])
    third = to_part(owned[0])
    shape = (plan.groups // 2, plan.parts)
    begun = stack(
        plan,
        [
            ([(got[chip], 0) for chip in plan.chips], shape + given[0].shape),
            ([(x, 0) for x in second], shape + second[0].shape),
            ([(x, 0) for x in third], (plan.parts,) + third[0].shape),
        ],
    )
    chunks = {number: [begun[number], over_grid(begun[number], 1)] for number in range(2)}
    from_part, two = {}, {2: [(x, 0) for x in to_chip(begun[2])]}

    def slices(first, last, x):
        parts, at = to_part(x), 0
        for number in range(first, last):
            from_part[number] = [(part, at) for part in parts]
            at += sizes[number]
        return parts[-1]

    marks = [slices(3, later, gate(owned[1], begun[2]))]
    before_first = []

    def advance(stage, mark):
        if stage == 1:
            slices(later, len(layouts), gate(owned[2], mark, marks[-1]))
        jobs, done = [], []
        if stage + 1 in two:
            shape = (plan.groups // 2, plan.parts, sizes[stage + 1]) + slab
            jobs.append((two[stage + 1], shape))
            done.append(stage + 1)
        if stage + 2 in from_part:
            jobs.append((from_part[stage + 2], (plan.parts, sizes[stage + 2]) + slab))
            done.append(stage + 2)
        for x, number in zip(stack(plan, jobs, mark) if jobs else [], done):
            if number == stage + 1:
                chunks[number] = [x, over_grid(x, 1)]
            else:
                two[number] = [(x, 0) for x in to_chip(x)]

    def matrices(level, wanted):
        (number,) = {where[name, level][0] for name in wanted}
        return chunks[number], {name: where[name, level][1] for name in wanted}

    full = (plan.parts, plan.kept, plan.groups, plan.rows, plan.width)
    slab_bytes = plan.slab[0] * plan.slab[1] * 2
    one_pass = 2 * plan.slab[0] * plan.slab[1] * plan.sources * plan.groups * max(1, owners // 4)

    forward_out, sent, starts, arrived, more = [], [], {}, [], None
    for level in range(levels):
        last, fresh = level == top, level == 0
        blocks, part_of = matrices(level, ["fwd", "inv" if last else "upd"])
        count = len(blocks)
        args, specs = [], []
        if not last and not fresh:
            args.append(keys)
            specs.append(VM)
        if not fresh:
            args += [starts[level]] + arrived
            specs += [VM] * (1 + owners)
        if more is not None and not last:
            args.append(more)
            specs.append(VM)
        args += blocks
        specs += [VM] * count
        if fresh:
            args += before_first
            specs += [UNREAD] * len(before_first)
        outs = [(plan.slab, F32)]
        if last:
            outs.append((plan.slab, BF))
        else:
            outs.append(((plan.slab[0], plan.update_rows), BF))
            outs += [(plan.slab, F32)] + [(plan.slab, BF)] * (owners - 1)
        if fresh:
            outs.append(((2, levels - 1, plan.groups, plan.sources), jnp.int32))
            outs += [(plan.slab, F32)] * top
        got = call(
            functools.partial(
                forward_kernel, plan, level, part_of, more is not None and not last,
                len(before_first),
            ),
            args, specs, outs, [], one_pass, 24 * slab_bytes,
        )
        forward_out.append(got[0])
        if last:
            solved = got[1]
            break
        sent.append(got[1])
        if fresh:
            keys = got[-1 - top]
            starts.update(zip(range(1, levels), got[-top:]))
        arrived = from_owners(got[2 : 2 + owners])
        advance(level, got[1])
        more = None
        if level + 1 == top:
            starts[top] = gate(starts[top], got[1], flops=100 * one_pass)
        if level + 1 < top:
            (more,) = call(
                functools.partial(ahead_kernel, plan, level + 1),
                sent + [keys], [VM] * (len(sent) + 1), [((owners,) + plan.slab, F32)], [],
                100 * one_pass * len(sent), 16 * slab_bytes,
            )

    solutions = {top: solved}
    everywhere = {}
    for level in reversed(range(top)):
        above = solutions[level + 1]
        everywhere[level + 1] = from_owners([above] * owners)
        froms = list(range(level + 2, levels))
        known = []
        if not froms:
            forward_out[level] = gate(forward_out[level], above, flops=100 * one_pass)
        if froms:
            slabs = sum([everywhere[f] for f in froms], [])
            known = call(
                functools.partial(known_kernel, plan, level, froms),
                [keys] + slabs, [VM] * (1 + len(slabs)),
                [((plan.groups, plan.chunk, plan.sources), BF)], [],
                100 * one_pass * len(froms), 16 * slab_bytes,
            )
        advance(levels + top - level - 2, above)
        blocks, part_of = matrices(level, ["upper", "inv"])
        args = [keys] + everywhere[level + 1] + list(known) + [forward_out[level]]
        (solutions[level],) = call(
            functools.partial(backward_kernel, plan, level, part_of, bool(froms)),
            args + blocks, [VM] * (len(args) + len(blocks)), [(plan.slab, BF)], [],
            one_pass, 24 * slab_bytes,
        )

    piece = ((levels + 1) // 2, plan.kept * plan.chunk, LANES)
    own = call(
        functools.partial(pieces_kernel, plan),
        [solutions[level] for level in range(levels)], [VM] * levels,
        [(piece, BF)] * len(plan.blocks), [], 1, 8 * slab_bytes,
    )
    far_first = sorted(range(len(plan.blocks)), key=lambda i: -sum(b.bit_count() for b in plan.blocks[i]))
    theirs = {i: swap(own[i], *plan.blocks[i]) for i in far_first}
    theirs = [theirs[i] for i in range(len(own))]
    (result,) = call(
        functools.partial(result_kernel, plan),
        theirs, [VM] * len(theirs), [(rhs.shape, BF)],
        [pltpu.VMEM(((levels + 1) // 2, plan.kept, plan.columns, LANES), BF)], 1, 8 * slab_bytes,
    )
    return result


def solution(mesh):
    def local(rhs, fwd_inv, bwd_inv, upd_t, bwd_t, dest_owner, dest_row):
        plan = Plan(mesh, rhs, upd_t, bwd_t)
        return solve(plan, rhs, fwd_inv, bwd_inv, upd_t, bwd_t, dest_owner, dest_row)

    rows = P(None, "leaf", "grid", None)
    placed = (rows, rows, rows, rows, rows, P(None, "leaf", "grid", None, None), rows)
    return jax.shard_map(local, mesh=mesh, in_specs=placed, out_specs=rows, check_vma=False)
```

```python
import functools

import jax
import jax.numpy as jnp
from jax import lax
from jax.experimental import pallas as pl
from jax.experimental.pallas import tpu as pltpu
from jax.sharding import PartitionSpec as P

BF = jnp.bfloat16
F32 = jnp.float32
LANES = 128
ROWS_AT_ONCE = 256
VMEM_BYTES = 16 * 1024 * 1024
PACK_VMEM_BYTES = 60 * 1024 * 1024


def nn(a, b):
    return lax.dot_general(a, b, (((1,), (0,)), ((), ())), preferred_element_type=F32)


def nt(a, b):
    return lax.dot_general(a, b, (((1,), (1,)), ((), ())), preferred_element_type=F32)


class Plan:
    def __init__(self, mesh, rhs, upd_t, bwd_t):
        self.levels, self.kept, self.rows, self.columns = rhs.shape
        self.leaves, self.groups = mesh.shape["leaf"], mesh.shape["grid"]
        self.parts = 2 if self.leaves % 2 == 0 else 1
        self.owners = self.leaves // self.parts
        self.supers = self.parts * self.kept
        self.chunk = self.columns // (self.groups * self.parts)
        self.width = self.rows * self.groups
        self.update_rows = upd_t.shape[3]
        self.group_rows = bwd_t.shape[2]
        self.slab = (self.supers * self.chunk, self.width)
        self.chips = [(dp, dg) for dg in range(0, self.groups, 2) for dp in range(self.parts)]
        self.shared = self.levels % 2 == 1
        self.coded = -(-3 * (self.levels - 1) // 16) * 16
        self.sources = self.supers * self.group_rows
        self.blocks = [(dp, dg) for dp in range(self.parts) for dg in range(self.groups)]

    def place(self):
        leaf, grid = lax.axis_index("leaf"), lax.axis_index("grid")
        return leaf // self.parts, leaf % self.parts, grid


def wait(group):
    for copy in group:
        copy.wait()


def block_of(plan, stacks, p, g, row):
    same = lax.axis_index("grid") % 2 == g % 2
    return jnp.where(same, stacks[0][g // 2, p, row], stacks[1][g // 2, p, row])


def joined(plan, stacks, slab, s, count=1):
    p, k = s // plan.kept, s % plan.kept
    rows = [
        block_of(plan, stacks, p, g, (slab + i) * plan.kept + k)
        for g in range(plan.groups)
        for i in range(count)
    ]
    return jnp.concatenate(rows, axis=0)


def start_slab(plan, stacks, first, level):
    low_core = lax.axis_index("grid") % 2 == 0

    def piece(p, g):
        both = block_of(plan, stacks, p, g, first + level // 2).astype(F32)
        return jnp.where(low_core, both[:, :LANES], both[:, LANES:])

    out = []
    for pair in range(plan.groups // 2):
        halves = [cross(piece(p, 2 * pair), piece(p, 2 * pair + 1))[level % 2] for p in range(plan.parts)]
        out.append(jnp.concatenate(halves, axis=0))
    return jnp.concatenate(out, axis=1)


def coded_lines(plan, stacks, p, g, end):
    if not plan.shared:
        return block_of(plan, stacks, p, g, end)[: plan.coded].astype(F32)
    both = block_of(plan, stacks, p, g, end - 1).astype(F32)
    lines = jnp.where(lax.axis_index("grid") % 2 == 0, both[:, :LANES], both[:, LANES:])
    low = lax.broadcasted_iota(jnp.int32, (plan.coded, LANES), 1) < LANES // 2
    out = []
    for i in range(0, 2 * plan.width // LANES, 2):
        one, two = [lines[(i + j) * plan.coded : (i + j + 1) * plan.coded] for j in range(2)]
        out.append(jnp.where(low, pltpu.roll(one, LANES // 2, 1), two))
    return jnp.concatenate(out, axis=1)


def copy_matrices(plan, sources, layout, target, sems, at):
    copies = []
    for i, (source, index) in enumerate(layout):
        to = target.at[pl.ds(i * plan.kept, plan.kept)]
        copies.append(pltpu.make_async_copy(sources[source].at[index], to, sems.at[at + i]))
        copies[-1].start()
    return copies


def pack_kernel(plan, layouts, *refs):
    sources, targets, sems = refs[:4], refs[-1 - len(layouts) : -1], refs[-1]
    copies = []
    for layout, target in zip(layouts, targets):
        copies += copy_matrices(plan, sources, layout, target, sems, len(copies))
    wait(copies)


def first_kernel(plan, layout, second, pairs, *refs):
    refs = list(refs)
    sources = [refs.pop(0) for _ in range(4)]
    rhs_ref, owner_ref, row_ref = [refs.pop(0) for _ in range(3)]
    firsts, second_ref = [refs.pop(0) for _ in plan.chips], refs.pop(0)
    raw_ref, turned_ref, sems = refs
    owner_at, part, grid = plan.place()
    k, r, c = plan.kept, plan.rows, plan.chunk
    fill = pltpu.make_async_copy(rhs_ref, raw_ref, sems.at[0])
    fill.start()
    copies = []
    for target in firsts:
        copies += copy_matrices(plan, sources, layout, target, sems, 1 + len(copies))
    copies += copy_matrices(plan, sources, second, second_ref, sems, 1 + len(copies))
    first = len(layout) * k
    leaf_to, row_to = [
        jnp.concatenate([ref[level, 0] for level in range(plan.levels - 1)], axis=0) for ref in (owner_ref, row_ref)
    ]
    block_to = row_to // r
    super_to = (block_to // k * plan.parts + leaf_to % plan.parts) * k + block_to % k
    fields = [(leaf_to // plan.parts) ^ owner_at, row_to % r, super_to]
    lines = [x[i : i + 1].astype(F32) for i in range(plan.levels - 1) for x in fields]
    lines.append(jnp.zeros((r - len(lines), plan.width), F32))
    shape = (plan.width, plan.width)
    now, then = lax.broadcasted_iota(jnp.int32, shape, 0), lax.broadcasted_iota(jnp.int32, shape, 1)
    move = jnp.where(now == then % plan.group_rows * k + then // plan.group_rows, 1.0, 0.0).astype(BF)
    lines = nn(jnp.concatenate(lines, axis=0).astype(BF), move).astype(BF)
    if plan.shared:
        lines = lines[: plan.coded].astype(F32)
        parts = []
        for i in range(0, plan.width, LANES):
            parts += [pltpu.roll(lines[:, i : i + LANES], LANES // 2, 1), lines[:, i : i + LANES]]
        lines = jnp.concatenate(parts, axis=0)
    else:
        for target in firsts:
            target[first + len(pairs)] = lines
    shape = (plan.columns, plan.columns)
    same = lax.broadcasted_iota(jnp.int32, shape, 0) == lax.broadcasted_iota(jnp.int32, shape, 1)
    same = jnp.where(same, 1.0, 0.0).astype(BF)
    fill.wait()
    for j, pair in enumerate(pairs):
        for s in range(k):
            two = [raw_ref[level, s] for level in pair]
            two += [jnp.zeros((r, plan.columns), BF)] * (2 - len(two))
            turned_ref[s] = nt(same, jnp.concatenate(two, axis=0)).astype(BF)
        for target, (dp, dg) in zip(firsts, plan.chips):
            for s in range(k):
                for core in range(2):
                    column = ((part ^ dp) * plan.groups + (grid ^ dg) // 2 * 2 + core) * c
                    piece = turned_ref[s, pl.ds(pl.multiple_of(column, c), c), :]
                    if plan.shared and j == len(pairs) - 1:
                        low = lax.broadcasted_iota(jnp.int32, piece.shape, 1) < LANES // 2
                        here = lines[s * c : (s + 1) * c]
                        piece = jnp.where(low, piece.astype(F32), here).astype(BF)
                    target[first + j, s * c : (s + 1) * c, core * LANES : (core + 1) * LANES] = piece
    wait(copies)


def onehot(keys, first, rows):
    iota = lax.broadcasted_iota(jnp.int32, (rows, keys.shape[1]), 0)
    return jnp.where(iota == keys - first, 1.0, 0.0).astype(BF)


def cross(even, odd):
    half = even.shape[1] // 2
    low = lax.broadcasted_iota(jnp.int32, even.shape, 1) < half
    return (
        jnp.where(low, even, pltpu.roll(odd, half, 1)),
        jnp.where(low, pltpu.roll(even, half, 1), odd),
    )


def owners_at_once(plan):
    return min(plan.owners, max(2, ROWS_AT_ONCE // plan.rows))


def scatter(plan, sent, key_ref, level, levels_to, emit):
    c, per = plan.chunk, owners_at_once(plan)
    for pair in range(plan.groups // 2):
        given = []
        for g in (2 * pair, 2 * pair + 1):
            lanes = slice(g * plan.group_rows, (g + 1) * plan.group_rows)
            whole = jnp.concatenate([sent[s * c : (s + 1) * c, lanes] for s in range(plan.supers)], axis=1)
            super_to = key_ref[1, level, g : g + 1, :]
            given.append(
                jnp.concatenate(
                    [
                        whole * jnp.where(super_to == to * plan.supers + s, 1.0, 0.0).astype(BF)
                        for to in levels_to
                        for s in range(plan.supers)
                    ],
                    axis=0,
                )
            )
        for first in range(0, plan.owners, per):
            even, odd = [
                nt(
                    given[i],
                    onehot(
                        key_ref[0, level, 2 * pair + i : 2 * pair + i + 1, :],
                        first * plan.rows,
                        per * plan.rows,
                    ),
                )
                for i in range(2)
            ]
            for j in range(0, per, 2):
                at = slice(j * plan.rows, (j + 2) * plan.rows)
                one, two = cross(even[:, at], odd[:, at])
                for i, to in enumerate(levels_to):
                    rows = slice(i * plan.slab[0], (i + 1) * plan.slab[0])
                    emit(to, first + j, pair, one[rows])
                    emit(to, first + j + 1, pair, two[rows])


def gather(plan, froms, key_ref, level, done):
    c, per = plan.chunk, owners_at_once(plan)
    for pair in range(plan.groups // 2):
        lanes = slice(pair * LANES, (pair + 1) * LANES)
        total = [None, None]
        for first in range(0, plan.owners, per):
            given = [[], []]
            for _, slabs in froms:
                got = [[], []]
                for d in range(first, first + per, 2):
                    halves = cross(slabs[d][:, lanes].astype(F32), slabs[d + 1][:, lanes].astype(F32))
                    for i in range(2):
                        got[i].append(halves[i])
                for i in range(2):
                    given[i].append(jnp.concatenate(got[i], axis=1).astype(BF))
            for i in range(2):
                g = 2 * pair + i
                keys = key_ref[0, level, g : g + 1, :]
                super_to = key_ref[1, level, g : g + 1, :]
                found = nn(
                    jnp.concatenate(given[i], axis=0), onehot(keys, first * plan.rows, per * plan.rows)
                )
                at = 0
                for level_from, _ in froms:
                    for s in range(plan.supers):
                        term = jnp.where(super_to == level_from * plan.supers + s, found[at : at + c], 0.0)
                        total[i] = term if total[i] is None else total[i] + term
                        at += c
        for i in range(2):
            done(2 * pair + i, total[i])


def gate_kernel(*refs):
    pass


def stack_kernel(plan, counts, *refs):
    _, part, grid = plan.place()
    refs = list(refs)
    given = [[(refs.pop(0), first) for first in firsts] for firsts in counts]
    for parts, out in zip(given, refs[len(refs) - len(counts) :]):
        for i, (ref, first) in enumerate(parts):
            if len(out.shape) > 4 and len(ref.shape) > 3:
                out[(grid // 2) ^ i] = ref[...]
            elif len(out.shape) > 4:
                out[(grid // 2) ^ (i // plan.parts), part ^ (i % plan.parts)] = ref[...]
            else:
                out[part ^ i] = ref[first : first + out.shape[1]]


def forward_kernel(plan, level, part_of, added, unread, *refs):
    refs = list(refs)
    last, fresh = level == plan.levels - 1, level == 0
    c, halves = plan.chunk, plan.update_rows // plan.width
    key_ref = None if last or fresh else refs.pop(0)
    if not fresh:
        start_ref, *arrived = [refs.pop(0) for _ in range(1 + plan.owners)]
    more_ref = refs.pop(0) if added else None
    blocks = [refs.pop(0) for _ in range(2)]
    if fresh:
        del refs[:unread]
    out_ref = refs.pop(0)
    if last:
        solved_ref = refs.pop(0)
    else:
        sent_ref = refs.pop(0)
        slab_refs = [refs.pop(0) for _ in range(plan.owners)]
    if fresh:
        key_ref = refs.pop(0)
        next_refs = [refs.pop(0) for _ in range(plan.levels - 1)]
        pairs = (plan.levels + 1) // 2
        first = blocks[0].shape[2] - (not plan.shared) - pairs
        block = start_slab(plan, blocks, first, 0)
    else:
        block = start_ref[...] - arrived[0][...]
        for ref in arrived[1:]:
            block = block - ref[...].astype(F32)
    block = block.astype(BF)
    solved = jnp.concatenate(
        [nt(block[s * c : (s + 1) * c], joined(plan, blocks, part_of["fwd"], s)) for s in range(plan.supers)], axis=0
    )
    out_ref[...] = solved
    lowered = solved.astype(BF)
    if last:
        for s in range(plan.supers):
            at = slice(s * c, (s + 1) * c)
            solved_ref[at, :] = nt(lowered[at], joined(plan, blocks, part_of["inv"], s)).astype(BF)
        return
    if fresh:
        coded = [
            [coded_lines(plan, blocks, p, g, first + pairs) for p in range(plan.parts)]
            for g in range(plan.groups)
        ]
        for to in range(plan.levels - 1):
            for g in range(plan.groups):
                distance, row, super_to = [
                    jnp.concatenate([x[3 * to + i : 3 * to + i + 1] for x in coded[g]], axis=1) for i in range(3)
                ]
                key_ref[0, to, g : g + 1, :] = (distance * plan.rows + row).astype(jnp.int32)
                key_ref[1, to, g : g + 1, :] = super_to.astype(jnp.int32)
    for s in range(plan.supers):
        at = slice(s * c, (s + 1) * c)
        for half in range(halves):
            lanes = slice(half * plan.width, (half + 1) * plan.width)
            sent_ref[at, lanes] = nn(lowered[at], joined(plan, blocks, part_of["upd"] + half, s)).astype(BF)

    def emit(to, distance, pair, value):
        lanes = slice(pair * LANES, (pair + 1) * LANES)
        if more_ref is not None:
            value = value + more_ref[distance, :, lanes]
        slab_refs[distance][:, lanes] = value.astype(slab_refs[distance].dtype)

    scatter(plan, sent_ref[...], key_ref, level, [level + 1], emit)
    if fresh:
        for i, ref in enumerate(next_refs):
            ref[...] = start_slab(plan, blocks, first, i + 1)


def ahead_kernel(plan, level, *refs):
    sent, key_ref, more_ref = refs[:level], refs[level], refs[level + 1]
    for i, ref in enumerate(sent):

        def emit(to, distance, pair, value, first=i == 0):
            lanes = slice(pair * LANES, (pair + 1) * LANES)
            if not first:
                value = value + more_ref[distance, :, lanes]
            more_ref[distance, :, lanes] = value

        scatter(plan, ref[...], key_ref, i, [level + 1], emit)


def known_kernel(plan, level, froms, *refs):
    key_ref, out_ref = refs[0], refs[-1]
    slabs = [refs[1 + i * plan.owners : 1 + (i + 1) * plan.owners] for i in range(len(froms))]

    def done(g, value):
        out_ref[g] = value.astype(BF)

    gather(plan, list(zip(froms, slabs)), key_ref, level, done)


def backward_kernel(plan, level, part_of, known, *refs):
    refs = list(refs)
    key_ref = refs.pop(0)
    slabs = [refs.pop(0) for _ in range(plan.owners)]
    known_ref = refs.pop(0) if known else None
    forward_ref, *blocks, solved_ref = refs
    c, tall = plan.chunk, plan.group_rows // plan.rows
    pulled = [None] * plan.groups

    def done(g, value):
        if known:
            value = value + known_ref[g].astype(F32)
        pulled[g] = value.astype(BF)

    gather(plan, [(level + 1, slabs)], key_ref, level, done)
    for s in range(plan.supers):
        at = slice(s * c, (s + 1) * c)
        lanes = slice(s * plan.group_rows, (s + 1) * plan.group_rows)
        whole = jnp.concatenate([p[:, lanes] for p in pulled], axis=1)
        upper = nn(whole, joined(plan, blocks[:2], part_of["upper"], s, tall))
        reduced = (forward_ref[at, :] - upper).astype(BF)
        solved_ref[at, :] = nt(reduced, joined(plan, blocks[2:], part_of["inv"], s)).astype(BF)


def pieces_kernel(plan, *refs):
    _, part, grid = plan.place()
    slabs, outs = refs[: plan.levels], refs[plan.levels :]
    rows, half = plan.kept * plan.chunk, plan.rows
    low = lax.broadcasted_iota(jnp.int32, (rows, LANES), 1) < half
    for out, (dp, dg) in zip(outs, plan.blocks):
        first = pl.multiple_of((part ^ dp) * rows, rows)
        lane = pl.multiple_of((grid ^ dg) * half // LANES * LANES, LANES)
        turn = (grid ^ dg) * half % LANES
        for i in range(0, plan.levels, 2):
            two = [slab[pl.ds(first, rows), pl.ds(lane, LANES)].astype(F32) for slab in slabs[i : i + 2]]
            one = pltpu.roll(two[0], turn, 1)
            if len(two) > 1:
                one = jnp.where(low, one, pltpu.roll(two[1], half - turn, 1))
            out[i // 2] = one.astype(BF)


def result_kernel(plan, *refs):
    _, part, grid = plan.place()
    refs = list(refs)
    scratch, out = refs.pop(), refs.pop()
    c = plan.chunk
    shape = (plan.rows, LANES)
    lane = lax.broadcasted_iota(jnp.int32, shape, 1)
    row = lax.broadcasted_iota(jnp.int32, shape, 0)
    picks = [jnp.where(lane == row + i * plan.rows, 1.0, 0.0).astype(BF) for i in range(2)]
    for k in range(plan.kept):
        for ref, (dp, dg) in zip(refs, plan.blocks):
            at = ((part ^ dp) * plan.groups + (grid ^ dg)) * c
            for i in range((plan.levels + 1) // 2):
                scratch[i, k, pl.ds(pl.multiple_of(at, c), c), :] = ref[i, k * c : (k + 1) * c, :]
    for level in range(plan.levels):
        for k in range(plan.kept):
            out[level, k] = nt(picks[level % 2], scratch[level // 2, k]).astype(BF)


VM = pl.BlockSpec(memory_space=pltpu.VMEM)
ANY = pl.BlockSpec(memory_space=pltpu.HBM)
UNREAD = pl.BlockSpec(memory_space=pl.ANY)


def call(body, args, specs, outs, scratch, flops, moved, vmem=VMEM_BYTES):
    return pl.pallas_call(
        body,
        in_specs=specs,
        out_specs=[VM] * len(outs),
        out_shape=[jax.ShapeDtypeStruct(shape, dtype) for shape, dtype in outs],
        scratch_shapes=scratch,
        compiler_params=pltpu.CompilerParams(vmem_limit_bytes=vmem),
        cost_estimate=pl.CostEstimate(flops=flops, bytes_accessed=moved, transcendentals=0),
    )(*args)


def gate(x, *others, flops=0):
    return pl.pallas_call(
        gate_kernel,
        in_specs=[UNREAD] * (1 + len(others)),
        out_specs=UNREAD,
        out_shape=jax.ShapeDtypeStruct(x.shape, x.dtype),
        input_output_aliases={0: 0},
        compiler_params=pltpu.CompilerParams(vmem_limit_bytes=2**20),
        cost_estimate=pl.CostEstimate(flops=flops, bytes_accessed=0, transcendentals=0),
    )(x, *others)


def stack(plan, jobs, *others):
    args = [x for parts, _ in jobs for x, _ in parts]
    return call(
        functools.partial(stack_kernel, plan, [[first for _, first in parts] for parts, _ in jobs]),
        args + list(others), [VM] * len(args) + [UNREAD] * len(others),
        [(shape, BF) for _, shape in jobs], [], 1, 2**19,
    )


def solve(plan, rhs, fwd_inv, bwd_inv, upd_t, bwd_t, dest_owner, dest_row):
    levels, owners = plan.levels, plan.owners
    owner_at, part, grid = plan.place()

    def over_leaf(x, step):
        return lax.ppermute(x, "leaf", [(i, i ^ step) for i in range(plan.leaves)])

    def over_grid(x, step):
        return lax.ppermute(x, "grid", [(i, i ^ step) for i in range(plan.groups)])

    def from_owners(x):
        got = {d: over_leaf(x[d], d * plan.parts) for d in reversed(range(1, owners))}
        return [x[0]] + [got[d] for d in range(1, owners)]

    def swap(x, dp, dg):
        if (dp, dg) == (0, 0):
            return x
        g = plan.groups
        moves = [(i, ((i // g) ^ dp) * g + ((i % g) ^ dg)) for i in range(plan.leaves * g)]
        return lax.ppermute(x, ("leaf", "grid"), moves)

    top, every = levels - 1, slice(None)
    halves = plan.update_rows // plan.width
    tall = plan.group_rows // plan.rows

    def parts_of(name, level):
        if name == "upd":
            return [(2, (level, every, every, pl.ds(h * plan.width, plan.width))) for h in range(halves)]
        if name == "upper":
            return [(3, (level, every, pl.ds(h * plan.rows, plan.rows))) for h in range(tall)]
        return [(dict(fwd=0, inv=1)[name], (level,))]

    names = [[("fwd", level), ("upd", level)] for level in range(top)]
    names.append([("fwd", top), ("inv", top), ("inv", top - 1)])
    names += [[("upper", level), ("inv", level - 1)][: 1 + (level > 0)] for level in reversed(range(top))]
    where, layouts = {}, []
    for number, chunk in enumerate(names):
        layouts.append([])
        for name, level in chunk:
            where[name, level] = (number, len(layouts[-1]))
            layouts[-1] += parts_of(name, level)
    pairs = [tuple(range(i, min(i + 2, levels))) for i in range(0, levels, 2)]
    slab = (plan.rows, plan.width)
    matrices_given = (fwd_inv, bwd_inv, upd_t, bwd_t)

    ways, extra = len(plan.chips), len(pairs) + (not plan.shared)
    *given, second = call(
        functools.partial(first_kernel, plan, layouts[0], layouts[1], pairs),
        [*matrices_given, rhs, dest_owner.reshape(dest_row.shape), dest_row],
        [ANY] * 5 + [VM] * 2,
        [((len(layouts[0]) * plan.kept + extra,) + slab, BF)] * ways
        + [((len(layouts[1]) * plan.kept,) + slab, BF)],
        [
            pltpu.VMEM(rhs.shape, BF),
            pltpu.VMEM((plan.kept, plan.columns, LANES), BF),
            pltpu.SemaphoreType.DMA((1 + ways * len(layouts[0]) + len(layouts[1]),)),
        ],
        1, 2**20, PACK_VMEM_BYTES,
    )
    sizes = [len(x) * plan.kept for x in layouts]
    later = levels + 1
    grouped = [layouts[2], sum(layouts[3:later], []), sum(layouts[later:], [])]
    owned = call(
        functools.partial(pack_kernel, plan, grouped),
        [*matrices_given, given[0]], [ANY] * 4 + [UNREAD],
        [((len(x) * plan.kept,) + slab, BF) for x in grouped],
        [pltpu.SemaphoreType.DMA((sum(len(x) for x in grouped),))],
        1, 2**20,
    )
    got = {chip: swap(x, *chip) for chip, x in zip(plan.chips, given)}
    def to_part(x):
        return [x] + [over_leaf(x, dp) for dp in range(1, plan.parts)]

    def to_chip(x):
        return [x] + [over_grid(x, dg) for dg in range(2, plan.groups, 2)]

    second = to_part(second)
    second = second + sum([[over_grid(x, dg) for x in second] for dg in range(2, plan.groups, 2)], [])
    third = to_part(owned[0])
    shape = (plan.groups // 2, plan.parts)
    begun = stack(
        plan,
        [
            ([(got[chip], 0) for chip in plan.chips], shape + given[0].shape),
            ([(x, 0) for x in second], shape + second[0].shape),
            ([(x, 0) for x in third], (plan.parts,) + third[0].shape),
        ],
    )
    chunks = {number: [begun[number], over_grid(begun[number], 1)] for number in range(2)}
    from_part, two = {}, {2: [(x, 0) for x in to_chip(begun[2])]}

    def slices(first, last, x):
        parts, at = to_part(x), 0
        for number in range(first, last):
            from_part[number] = [(part, at) for part in parts]
            at += sizes[number]
        return parts[-1]

    marks = [slices(3, later, gate(owned[1], begun[2]))]
    before_first = []

    def advance(stage, mark):
        if stage == 1:
            slices(later, len(layouts), gate(owned[2], mark, marks[-1]))
        jobs, done = [], []
        if stage + 1 in two:
            shape = (plan.groups // 2, plan.parts, sizes[stage + 1]) + slab
            jobs.append((two[stage + 1], shape))
            done.append(stage + 1)
        if stage + 2 in from_part:
            jobs.append((from_part[stage + 2], (plan.parts, sizes[stage + 2]) + slab))
            done.append(stage + 2)
        for x, number in zip(stack(plan, jobs, mark) if jobs else [], done):
            if number == stage + 1:
                chunks[number] = [x, over_grid(x, 1)]
            else:
                two[number] = [(x, 0) for x in to_chip(x)]

    def matrices(level, wanted):
        (number,) = {where[name, level][0] for name in wanted}
        return chunks[number], {name: where[name, level][1] for name in wanted}

    full = (plan.parts, plan.kept, plan.groups, plan.rows, plan.width)
    slab_bytes = plan.slab[0] * plan.slab[1] * 2
    one_pass = 2 * plan.slab[0] * plan.slab[1] * plan.sources * plan.groups * max(1, owners // 4)

    forward_out, sent, starts, arrived, more = [], [], {}, [], None
    for level in range(levels):
        last, fresh = level == top, level == 0
        blocks, part_of = matrices(level, ["fwd", "inv" if last else "upd"])
        count = len(blocks)
        args, specs = [], []
        if not last and not fresh:
            args.append(keys)
            specs.append(VM)
        if not fresh:
            args += [starts[level]] + arrived
            specs += [VM] * (1 + owners)
        if more is not None and not last:
            args.append(more)
            specs.append(VM)
        args += blocks
        specs += [VM] * count
        if fresh:
            args += before_first
            specs += [UNREAD] * len(before_first)
        outs = [(plan.slab, F32)]
        if last:
            outs.append((plan.slab, BF))
        else:
            outs.append(((plan.slab[0], plan.update_rows), BF))
            outs += [(plan.slab, F32)] + [(plan.slab, BF)] * (owners - 1)
        if fresh:
            outs.append(((2, levels - 1, plan.groups, plan.sources), jnp.int32))
            outs += [(plan.slab, F32)] * top
        got = call(
            functools.partial(
                forward_kernel, plan, level, part_of, more is not None and not last,
                len(before_first),
            ),
            args, specs, outs, [], one_pass, 24 * slab_bytes,
        )
        forward_out.append(got[0])
        if last:
            solved = got[1]
            break
        sent.append(got[1])
        if fresh:
            keys = got[-1 - top]
            starts.update(zip(range(1, levels), got[-top:]))
        arrived = from_owners(got[2 : 2 + owners])
        advance(level, got[1])
        more = None
        if level + 1 == top:
            starts[top] = gate(starts[top], got[1], flops=100 * one_pass)
        if level + 1 < top:
            (more,) = call(
                functools.partial(ahead_kernel, plan, level + 1),
                sent + [keys], [VM] * (len(sent) + 1), [((owners,) + plan.slab, F32)], [],
                100 * one_pass * len(sent), 16 * slab_bytes,
            )

    solutions = {top: solved}
    everywhere = {}
    for level in reversed(range(top)):
        above = solutions[level + 1]
        everywhere[level + 1] = from_owners([above] * owners)
        froms = list(range(level + 2, levels))
        known = []
        if not froms:
            forward_out[level] = gate(forward_out[level], above, flops=100 * one_pass)
        if froms:
            slabs = sum([everywhere[f] for f in froms], [])
            known = call(
                functools.partial(known_kernel, plan, level, froms),
                [keys] + slabs, [VM] * (1 + len(slabs)),
                [((plan.groups, plan.chunk, plan.sources), BF)], [],
                100 * one_pass * len(froms), 16 * slab_bytes,
            )
        advance(levels + top - level - 2, above)
        blocks, part_of = matrices(level, ["upper"])
        inverses, inverse_part = matrices(level, ["inv"])
        blocks, part_of = blocks + inverses, dict(part_of, **inverse_part)
        args = [keys] + everywhere[level + 1] + list(known) + [forward_out[level]]
        (solutions[level],) = call(
            functools.partial(backward_kernel, plan, level, part_of, bool(froms)),
            args + blocks, [VM] * (len(args) + len(blocks)), [(plan.slab, BF)], [],
            one_pass, 24 * slab_bytes,
        )

    piece = ((levels + 1) // 2, plan.kept * plan.chunk, LANES)
    own = call(
        functools.partial(pieces_kernel, plan),
        [solutions[level] for level in range(levels)], [VM] * levels,
        [(piece, BF)] * len(plan.blocks), [], 1, 8 * slab_bytes,
    )
    far_first = sorted(range(len(plan.blocks)), key=lambda i: -sum(b.bit_count() for b in plan.blocks[i]))
    theirs = {i: swap(own[i], *plan.blocks[i]) for i in far_first}
    theirs = [theirs[i] for i in range(len(own))]
    (result,) = call(
        functools.partial(result_kernel, plan),
        theirs, [VM] * len(theirs), [(rhs.shape, BF)],
        [pltpu.VMEM(((levels + 1) // 2, plan.kept, plan.columns, LANES), BF)], 1, 8 * slab_bytes,
    )
    return result


def solution(mesh):
    def local(rhs, fwd_inv, bwd_inv, upd_t, bwd_t, dest_owner, dest_row):
        plan = Plan(mesh, rhs, upd_t, bwd_t)
        return solve(plan, rhs, fwd_inv, bwd_inv, upd_t, bwd_t, dest_owner, dest_row)

    rows = P(None, "leaf", "grid", None)
    placed = (rows, rows, rows, rows, rows, P(None, "leaf", "grid", None, None), rows)
    return jax.shard_map(local, mesh=mesh, in_specs=placed, out_specs=rows, check_vma=False)
```
